768 devices in a mesh: context: 24 (over z, core), dp: 4 (over x), tensor: 8 (over y).
Axes of the slice: x: 4, y: 8, z: 12, core: 2. Of those that a mesh axis runs over, the one named last changes fastest.
Arguments:
- query_rows: bfloat16 [4, 3072, 4096], P('dp', 'context', 'tensor'), may hold values from -6 to 6
- key_rows: bfloat16 [4, 3072, 4096], P('dp', 'context', 'tensor'), may hold values from -6 to 6
- value_rows: bfloat16 [4, 3072, 4096], P('dp', 'context', 'tensor'), may hold values from -6 to 6
- out_weight: bfloat16 [4096, 6144], P('tensor', 'dp'), may hold values from -0.125 to 0.125
- grad_out: bfloat16 [4, 3072, 6144], P('dp', 'context'), may hold values from -4 to 4
Outputs:
- attended: bfloat16 [4, 3072, 6144], P('dp', 'context', 'tensor')
- grad_query: bfloat16 [4, 3072, 4096], P('dp', 'context', 'tensor')
- grad_key: bfloat16 [4, 3072, 4096], P('dp', 'context', 'tensor')
- grad_value: bfloat16 [4, 3072, 4096], P('dp', 'context', 'tensor')
The draws below stay inside these ranges and needn't reach their ends.
All inputs are finite; a program needn't handle non-finite values.
Results may differ from the reference program's by a relative error of at most 0.025.
Values may be sent and summed in bfloat16 or wider, within the bound.
A program may use at most 64 MiB of HBM per device.

```python
import jax
import jax.numpy as jnp
from jax import lax

D = 6144
DH = 128
HEADS = 32
TOK_DEV = 128
HD = 4096
LENGTH = 3072
SEQS = 4
N_CONTEXT = 24
N_TENSOR = 8


def strengthened(values, stream_key, source, target, blocks, factor):
    def block_of(position):
        return (jnp.arange(values.shape[position]) // (values.shape[position] // blocks)).reshape((-1,) + (1,) * (values.ndim - 1 - position))

    one_side = jax.random.permutation(stream_key, blocks)[block_of(target)]
    other_side = (block_of(target) + blocks // 2) % blocks
    return jnp.where((block_of(source) == one_side) | (block_of(source) == other_side), factor * values, values)


def shard_levels(stream_key, dims, cuts, low, top_value):
    factor_of = 1.0
    for axis_at, parts in cuts:
        steps = jax.random.uniform(jax.random.fold_in(jax.random.fold_in(stream_key, 6), axis_at), (parts,), jnp.float32, low / len(cuts), top_value / len(cuts))
        factor_of = factor_of * jnp.repeat(jnp.exp(steps), dims[axis_at] // parts).reshape((-1,) + (1,) * (len(dims) - 1 - axis_at))
    return factor_of


def normal_values(own_key, dims, width, bound, cuts=(), dtype=jnp.bfloat16):
    values = jax.random.normal(own_key, dims, jnp.float32) * width
    if len(cuts) > 0:
        values = shard_levels(own_key, dims, cuts, -0.22, 0.18) * values
    return jnp.clip(values, min=-bound, max=bound).astype(dtype)


def heavy_noise(rng, extent, width, bound, cuts, heavy, dtype=jnp.bfloat16):
    drawn = width * jax.random.normal(rng, extent, jnp.float32)
    if cuts:
        drawn = drawn * shard_levels(rng, extent, cuts, -0.22, 0.18)
    return jnp.clip(strengthened(drawn, jax.random.fold_in(rng, 3), *heavy), -bound, bound).astype(dtype)


def setup_inputs(seed: int = 0) -> dict:
    key_list = jax.random.split(jax.random.key(seed), 6)
    query_rows = normal_values(key_list[0], (SEQS, LENGTH, HD), 1.0, 6.0, ((0, 4), (1, 24), (2, 8)))
    key_rows = normal_values(key_list[1], (SEQS, LENGTH, HD), 1.0, 6.0, ((0, 4), (1, 24), (2, 8)))
    value_rows = normal_values(key_list[2], (SEQS, LENGTH, HD), 1.0, 6.0, ((0, 4), (1, 24), (2, 8)))
    out_weight = heavy_noise(key_list[3], (HD, D), HD ** -0.5, 0.125, ((0, 8), (1, 4)), (0, 1, 8, 2.0))
    grad_out = normal_values(key_list[4], (SEQS, LENGTH, D), 0.5, 4.0, ((0, 4), (1, 24)))
    return dict(query_rows=query_rows, key_rows=key_rows, value_rows=value_rows, out_weight=out_weight, grad_out=grad_out)


def causal_tri(size):
    places = jnp.arange(size)
    return (places[:, None] >= places[None, :]).astype(jnp.float32)


def one_sequence(query_f, key_f, value_f, grad_f):
    factor = (DH * LENGTH) ** -0.5
    precise = lax.Precision.HIGHEST
    causal = causal_tri(TOK_DEV)

    def blocks(array):
        return array.reshape(N_CONTEXT, TOK_DEV, HEADS, DH)

    q_all, k_all, v_all, g_all = blocks(query_f), blocks(key_f), blocks(value_f), blocks(grad_f)

    def forward_step(state, pieces):
        q_blk, k_blk, v_blk, g_blk = pieces
        scores = jnp.einsum('bhd,chd->hbc', q_blk, k_blk, precision=precise) * causal
        attn_out = factor * (jnp.einsum('hbc,che->bhe', scores, v_blk, precision=precise)
                             + jnp.einsum('bhd,hde->bhe', q_blk, state, precision=precise))
        d_scores = jnp.einsum('bhe,che->hbc', g_blk, v_blk, precision=precise) * causal
        grad_q = factor * (jnp.einsum('hbc,chd->bhd', d_scores, k_blk, precision=precise)
                           + jnp.einsum('bhe,hde->bhd', g_blk, state, precision=precise))
        state = state + jnp.einsum('chd,che->hde', k_blk, v_blk, precision=precise)
        return state, (attn_out, grad_q)

    def backward_step(state, pieces):
        q_blk, k_blk, v_blk, g_blk = pieces
        scores = jnp.einsum('bhd,chd->hbc', q_blk, k_blk, precision=precise) * causal
        d_scores = jnp.einsum('bhe,che->hbc', g_blk, v_blk, precision=precise) * causal
        state = state + jnp.einsum('bhd,bhe->hde', q_blk, g_blk, precision=precise)
        grad_k = factor * (jnp.einsum('hbc,bhd->chd', d_scores, q_blk, precision=precise)
                           + jnp.einsum('che,hde->chd', v_blk, state - jnp.einsum('bhd,bhe->hde', q_blk, g_blk, precision=precise), precision=precise))
        grad_v = factor * (jnp.einsum('hbc,bhe->che', scores, g_blk, precision=precise)
                           + jnp.einsum('chd,hde->che', k_blk, state - jnp.einsum('bhd,bhe->hde', q_blk, g_blk, precision=precise), precision=precise))
        return state, (grad_k, grad_v)

    start_state = jnp.zeros((HEADS, DH, DH), jnp.float32)
    _, (attn_out, grad_q) = lax.scan(forward_step, start_state, (q_all, k_all, v_all, g_all))
    _, (grad_k, grad_v) = lax.scan(backward_step, start_state, (q_all, k_all, v_all, g_all), reverse=True)
    flat = lambda array: array.reshape(LENGTH, HD)
    return flat(attn_out), flat(grad_q), flat(grad_k), flat(grad_v)


def reference(query_rows, key_rows, value_rows, out_weight, grad_out):
    grad_attn = jnp.dot(grad_out.reshape(SEQS * LENGTH, D), out_weight.T,
                        preferred_element_type=jnp.float32).astype(jnp.bfloat16)
    grad_attn = grad_attn.reshape(SEQS, LENGTH, HD)
    attn_out, grad_q, grad_k, grad_v = jax.vmap(one_sequence)(
        query_rows.astype(jnp.float32), key_rows.astype(jnp.float32),
        value_rows.astype(jnp.float32), grad_attn.astype(jnp.float32))
    attn_flat = attn_out.astype(jnp.bfloat16).reshape(SEQS * LENGTH, HD)
    group_width = HD // N_TENSOR
    attended = jnp.zeros((SEQS * LENGTH, D), jnp.float32)
    for group in range(N_TENSOR):
        partial_out = jnp.dot(attn_flat[:, group * group_width:(group + 1) * group_width],
                              out_weight[group * group_width:(group + 1) * group_width],
                              preferred_element_type=jnp.float32)
        attended = attended + partial_out.astype(jnp.bfloat16).astype(jnp.float32)
    attended = attended.astype(jnp.bfloat16).reshape(SEQS, LENGTH, D)
    return (attended, grad_q.astype(jnp.bfloat16), grad_k.astype(jnp.bfloat16), grad_v.astype(jnp.bfloat16))
```

```python
import functools

import jax
import jax.numpy as jnp
from jax import lax
from jax.experimental import pallas as pl
from jax.experimental.pallas import tpu as pltpu
from jax.sharding import PartitionSpec as P

DH = 128
BF = jnp.bfloat16
F32 = jnp.float32
MESH = pl.DeviceIdType.MESH


def dot(a, b, ca, cb):
    return lax.dot_general(a, b, (((ca,), (cb,)), ((), ())), preferred_element_type=F32)


def kernel(
    sizes, q_hbm, k_hbm, v_hbm, w_hbm, go_hbm, att_ref, dq_ref, dk_ref, dv_ref,
    q_ref, k_ref, v_ref, panel, go, grad_acc, attn32, attn16, part, y_in,
    local_kv, local_qd, got_kv, got_qd, tot_kv, tot_qd, far_kv, far_qd,
    out_kv, out_qd, prefix, suffix, send_sem, recv_sem, load_sem,
):
    n_ctx, n_x, n_y, factor = sizes
    rows, width = q_ref.shape
    heads = width // DH
    wide = panel.shape[2]
    c, x, y = lax.axis_index("context"), lax.axis_index("dp"), lax.axis_index("tensor")
    core, z = lax.rem(c, 2), c // 2
    parity = lax.rem(z, 2)
    member, group = lax.rem(c, 8), c // 8
    n_groups = n_ctx // 8

    def at_ctx(i):
        return {"context": lax.rem(i + n_ctx, n_ctx)}

    right_x, left_x = {"dp": lax.rem(x + 1, n_x)}, {"dp": lax.rem(x + n_x - 1, n_x)}
    up_y, down_y = {"tensor": lax.rem(y + 1, n_y)}, {"tensor": lax.rem(y + n_y - 1, n_y)}
    up_z, down_z = at_ctx(c + 2), at_ctx(c - 2)
    sibling = {"context": c + 1 - 2 * core}

    def mate(i):
        return {"context": c - member + i}

    barrier = pltpu.get_barrier_semaphore()
    peers = [right_x, left_x, up_y, down_y, up_z, down_z]
    peers += [mate(lax.rem(member + o, 8)) for o in range(1, 8)]
    peers += [at_ctx(c + 8 * o) for o in range(1, n_groups)]
    for peer in peers:
        pl.semaphore_signal(barrier, inc=1, device_id=peer, device_id_type=MESH)

    loads = []

    def load(src, dst):
        copy = pltpu.make_async_copy(src, dst, load_sem.at[len(loads)])
        copy.start()
        loads.append(copy)
        return copy

    load_k = load(k_hbm.at[0], k_ref)
    load_v = load(v_hbm.at[0], v_ref)
    load_q = load(q_hbm.at[0], q_ref)
    load_w = load(w_hbm, panel.at[0])
    load_go = []
    for r in range(n_x):
        columns = pl.ds(pl.multiple_of(lax.rem(x + r, n_x) * wide, wide), wide)
        load_go.append(load(go_hbm.at[0, :, columns], go.at[r]))
    pl.semaphore_wait(barrier, len(peers))

    sent = []

    def send(src, dst, here, device):
        i = len(sent)
        copy = pltpu.make_async_remote_copy(
            src, dst, send_sem.at[i], recv_sem.at[i], device, MESH
        )
        copy.start()
        sent.append(copy)
        landing = pltpu.make_async_remote_copy(
            src, here, send_sem.at[i], recv_sem.at[i], device, MESH
        )
        return landing.wait_recv

    def piece(ref, par, cor, d):
        start = pl.multiple_of(par * 256 + cor * 128 + d * 64, 64)
        return ref.at[pl.ds(start, 64)]

    def mine(ref, d):
        return piece(ref, parity, core, d)

    def x_send(src, r, d, device):
        dst = mine(panel.at[r], d)
        return send(src, dst, dst, device)

    x_got = {}
    x_got[3, 0] = x_send(mine(w_hbm, 0), 3, 0, right_x)
    x_got[1, 1] = x_send(mine(w_hbm, 1), 1, 1, left_x)
    x_got[3, 1] = x_send(mine(w_hbm, 1), 3, 1, right_x)
    x_got[1, 0] = x_send(mine(w_hbm, 0), 1, 0, left_x)
    z_got, pass_x, pass_z = {}, {}, {}

    def on_x(r, d):
        x_got[r, d]()
        block = mine(panel.at[r], d)
        if (r, d) == (3, 0):
            x_got[2, 0] = x_send(block, 2, 0, right_x)
        if (r, d) == (1, 1):
            x_got[2, 1] = x_send(block, 2, 1, left_x)
        other = piece(panel.at[r], 1 - parity, core, d)
        z_got[r, d] = send(block, block, other, up_z if d == 0 else down_z)
        theirs = piece(panel.at[r], parity, 1 - core, d)
        pass_x[r, d] = send(block, block, theirs, sibling)

    def on_z(r, d):
        z_got[r, d]()
        block = piece(panel.at[r], 1 - parity, core, d)
        theirs = piece(panel.at[r], 1 - parity, 1 - core, d)
        pass_z[r, d] = send(block, block, theirs, sibling)

    def slot_done(r):
        for d in range(2):
            pass_x[r, d]()
            pass_z[r, d]()

    def part_of(ref, i):
        return ref.at[pl.ds(pl.multiple_of(i * 64, 64), 64)]

    def spread(local, got):
        waits = []
        for o in range(1, 8):
            to, source = lax.rem(member + o, 8), lax.rem(member + 8 - o, 8)
            waits.append(
                send(part_of(local, to), part_of(got, member), part_of(got, source), mate(to))
            )
        part_of(got, member)[...] = part_of(local, member)[...]
        return waits

    def totals(waits, got, tot, far):
        for wait in waits:
            wait()
        tot[...] = sum(got[i * 64 : i * 64 + 64].astype(F32) for i in range(8)).astype(BF)
        return [
            send(tot, far.at[o - 1], far.at[o - 1], at_ctx(c + 8 * o))
            for o in range(1, n_groups)
        ]

    def scan(waits, got, far, out, state, reverse):
        running = jnp.zeros((64, DH), F32)
        for o in range(1, n_groups):
            waits[o - 1]()
            earlier = group >= o
            keep = jnp.where(earlier, 0.0, 1.0) if reverse else jnp.where(earlier, 1.0, 0.0)
            running = running + keep.astype(F32) * far[o - 1].astype(F32)
        for i in reversed(range(8)) if reverse else range(8):
            out[i * 64 : i * 64 + 64] = running.astype(BF)
            running = running + got[i * 64 : i * 64 + 64].astype(F32)
        waits = []
        for o in range(1, 8):
            to, source = lax.rem(member + o, 8), lax.rem(member + 8 - o, 8)
            waits.append(
                send(part_of(out, to), part_of(state, member), part_of(state, source), mate(to))
            )
        part_of(state, member)[...] = part_of(out, member)[...]
        return waits

    def head(ref, h):
        return ref[:, h * DH : (h + 1) * DH]

    def state_of(ref, h):
        return ref[h * DH : (h + 1) * DH, :]

    first = lax.broadcasted_iota(jnp.int32, (rows, rows), 0)
    second = lax.broadcasted_iota(jnp.int32, (rows, rows), 1)
    causal = (first >= second).astype(F32)
    causal_t = (first <= second).astype(F32)

    load_k.wait()
    load_v.wait()
    for h in range(heads):
        local_kv[h * DH : (h + 1) * DH, :] = dot(head(k_ref, h), head(v_ref, h), 0, 0).astype(BF)
    kv_waits = spread(local_kv, got_kv)

    load_q.wait()
    for h in range(heads):
        scores = (dot(head(q_ref, h), head(k_ref, h), 1, 1) * causal).astype(BF)
        attn32[:, h * DH : (h + 1) * DH] = dot(scores, head(v_ref, h), 1, 0)

    kv_waits = totals(kv_waits, got_kv, tot_kv, far_kv)
    load_w.wait()
    load_go[0].wait()
    grad_acc[...] = dot(go[0], panel[0], 1, 1)

    kv_waits = scan(kv_waits, got_kv, far_kv, out_kv, prefix, False)
    on_x(3, 0)
    on_x(1, 1)
    for wait in kv_waits:
        wait()
    for h in range(heads):
        total = attn32[:, h * DH : (h + 1) * DH] + dot(head(q_ref, h), state_of(prefix, h), 1, 0)
        attn16[:, h * DH : (h + 1) * DH] = (factor * total).astype(BF)

    half = wide // 4

    def project(r):
        for i in range(4):
            part[r * 4 + i] = dot(
                attn16[...], panel[r, :, i * half : (i + 1) * half], 1, 0
            ).astype(BF)

    project(0)
    on_x(3, 1)
    on_x(1, 0)
    on_z(3, 0)
    on_z(1, 1)
    on_x(2, 0)
    on_x(2, 1)
    on_z(3, 1)
    on_z(1, 0)
    for r in (3, 1):
        slot_done(r)
        load_go[r].wait()
        grad_acc[...] += dot(go[r], panel[r], 1, 1)
        project(r)
    on_z(2, 0)
    on_z(2, 1)
    slot_done(2)
    load_go[2].wait()

    def chunk_of(to, which):
        slot = lax.rem(to // 2 + n_x - x, n_x)
        return slot * 4 + lax.rem(to, 2) * 2 + which

    distance = (4, 3, 3, 2, 2, 1, 1)
    y_got = ([], [])

    def y_step(j):
        for way in range(2):
            to = lax.rem(y + (distance[j] if way == 0 else n_y - distance[j]), n_y)
            chunk = chunk_of(to, (j + way) % 2)
            if j >= 2:
                y_got[way][j - 2]()
                total = part[chunk].astype(F32) + y_in[way * 7 + j - 2].astype(F32)
                part[chunk] = total.astype(BF)
            landing = y_in.at[way * 7 + j]
            y_got[way].append(
                send(part.at[chunk], landing, landing, up_y if way == 0 else down_y)
            )

    project(2)
    y_step(0)
    y_step(1)
    grads = (grad_acc[...] + dot(go[2], panel[2], 1, 1)).astype(BF)
    g_heads = [grads[:, h * DH : (h + 1) * DH] for h in range(heads)]
    for h in range(heads):
        local_qd[h * DH : (h + 1) * DH, :] = dot(head(q_ref, h), g_heads[h], 0, 0).astype(BF)
    qd_waits = spread(local_qd, got_qd)
    y_step(2)
    qd_waits = totals(qd_waits, got_qd, tot_qd, far_qd)
    y_step(3)
    for h in range(heads):
        own = slice(h * DH, (h + 1) * DH)
        d_scores = (dot(g_heads[h], head(v_ref, h), 1, 1) * causal).astype(BF)
        total = dot(d_scores, head(k_ref, h), 1, 0) + dot(g_heads[h], state_of(prefix, h), 1, 1)
        dq_ref[0, :, own] = (factor * total).astype(BF)
    qd_waits = scan(qd_waits, got_qd, far_qd, out_qd, suffix, True)
    y_step(4)
    for wait in qd_waits:
        wait()
    for h in range(heads):
        own = slice(h * DH, (h + 1) * DH)
        d_scores = (dot(head(v_ref, h), g_heads[h], 1, 1) * causal_t).astype(BF)
        total = dot(d_scores, head(q_ref, h), 1, 0) + dot(head(v_ref, h), state_of(suffix, h), 1, 1)
        dk_ref[0, :, own] = (factor * total).astype(BF)
        scores = (dot(head(k_ref, h), head(q_ref, h), 1, 1) * causal_t).astype(BF)
        total = dot(scores, g_heads[h], 1, 0) + dot(head(k_ref, h), state_of(suffix, h), 1, 0)
        dv_ref[0, :, own] = (factor * total).astype(BF)
    y_step(5)
    y_step(6)
    for which in range(2):
        up, down = 6 - which, 5 + which
        y_got[0][up]()
        y_got[1][down]()
        total = part[chunk_of(y, which)].astype(F32)
        total = total + y_in[up].astype(F32) + y_in[7 + down].astype(F32)
        att_ref[0, :, which * half : (which + 1) * half] = total.astype(BF)
    for copy in sent:
        copy.wait_send()


def solution(mesh):
    n_ctx, n_x, n_y = mesh.shape["context"], mesh.shape["dp"], mesh.shape["tensor"]

    def shards(q, k, v, w, go):
        _, rows, width = q.shape
        depth, wide = w.shape
        factor = float(DH * rows * n_ctx) ** (-0.5)
        states = width // DH * DH
        half = wide // 4
        sizes = (n_ctx, n_x, n_y, factor)
        head_out = jax.ShapeDtypeStruct((1, rows, width), BF)
        state = pltpu.VMEM((states, DH), BF)
        total = pltpu.VMEM((states // 8, DH), BF)
        far = pltpu.VMEM((2, states // 8, DH), BF)
        return pl.pallas_call(
            functools.partial(kernel, sizes),
            out_shape=(
                jax.ShapeDtypeStruct((1, rows, n_x * wide // n_y), BF),
                head_out,
                head_out,
                head_out,
            ),
            in_specs=[pl.BlockSpec(memory_space=pl.ANY)] * 5,
            out_specs=[pl.BlockSpec(memory_space=pltpu.VMEM)] * 4,
            scratch_shapes=[
                pltpu.VMEM((rows, width), BF),
                pltpu.VMEM((rows, width), BF),
                pltpu.VMEM((rows, width), BF),
                pltpu.VMEM((n_x, depth, wide), BF),
                pltpu.VMEM((n_x, rows, wide), BF),
                pltpu.VMEM((rows, width), F32),
                pltpu.VMEM((rows, width), F32),
                pltpu.VMEM((rows, width), BF),
                pltpu.VMEM((4 * n_x, rows, half), BF),
                pltpu.VMEM((14, rows, half), BF),
                state, state, state, state, total, total, far, far,
                state, state, state, state,
                pltpu.SemaphoreType.DMA((70,)),
                pltpu.SemaphoreType.DMA((70,)),
                pltpu.SemaphoreType.DMA((8,)),
            ],
            compiler_params=pltpu.CompilerParams(
                collective_id=0, has_side_effects=True, vmem_limit_bytes=56 << 20
            ),
        )(q, k, v, w, go)

    rows_spec = P("dp", "context", "tensor")
    return jax.shard_map(
        shards,
        mesh=mesh,
        in_specs=(rows_spec, rows_spec, rows_spec, P("tensor", "dp"), P("dp", "context", None)),
        out_specs=(rows_spec,) * 4,
        check_vma=False,
    )
```

```python
import functools

import jax
import jax.numpy as jnp
from jax import lax
from jax.experimental import pallas as pl
from jax.experimental.pallas import tpu as pltpu
from jax.sharding import PartitionSpec as P

DH = 128
BF = jnp.bfloat16
F32 = jnp.float32
MESH = pl.DeviceIdType.MESH


def dot(a, b, ca, cb):
    return lax.dot_general(a, b, (((ca,), (cb,)), ((), ())), preferred_element_type=F32)


def kernel(
    sizes, q_hbm, k_hbm, v_hbm, w_hbm, go_hbm, att_ref, dq_ref, dk_ref, dv_ref,
    q_ref, k_ref, v_ref, panel, go, grad_acc, attn32, attn16, part, y_in,
    local_kv, local_qd, got_kv, got_qd, tot_kv, tot_qd, far_kv, far_qd,
    out_kv, out_qd, prefix, suffix, send_sem, recv_sem, load_sem,
):
    n_ctx, n_x, n_y, factor = sizes
    rows, width = q_ref.shape
    heads = width // DH
    depth, wide = panel.shape[1:]
    c, x, y = lax.axis_index("context"), lax.axis_index("dp"), lax.axis_index("tensor")
    core, z = lax.rem(c, 2), c // 2
    parity = lax.rem(z, 2)
    member, group = lax.rem(c, 8), c // 8
    n_groups = n_ctx // 8

    def at_ctx(i):
        return {"context": lax.rem(i + n_ctx, n_ctx)}

    right_x, left_x = {"dp": lax.rem(x + 1, n_x)}, {"dp": lax.rem(x + n_x - 1, n_x)}
    up_y, down_y = {"tensor": lax.rem(y + 1, n_y)}, {"tensor": lax.rem(y + n_y - 1, n_y)}
    up_z, down_z = at_ctx(c + 2), at_ctx(c - 2)
    sibling = {"context": c + 1 - 2 * core}

    def mate(i):
        return {"context": c - member + i}

    barrier = pltpu.get_barrier_semaphore()
    peers = [right_x, left_x, up_y, down_y, up_z, down_z]
    peers += [mate(lax.rem(member + o, 8)) for o in range(1, 8)]
    peers += [at_ctx(c + 8 * o) for o in range(1, n_groups)]
    for peer in peers:
        pl.semaphore_signal(barrier, inc=1, device_id=peer, device_id_type=MESH)

    loads = []

    def load(src, dst):
        copy = pltpu.make_async_copy(src, dst, load_sem.at[len(loads)])
        copy.start()
        loads.append(copy)
        return copy

    load_k = load(k_hbm.at[0], k_ref)
    load_v = load(v_hbm.at[0], v_ref)
    load_q = load(q_hbm.at[0], q_ref)
    load_w = load(w_hbm, panel.at[0])
    load_go = []
    for r in range(n_x):
        columns = pl.ds(pl.multiple_of(lax.rem(x + r, n_x) * wide, wide), wide)
        load_go.append(load(go_hbm.at[0, :, columns], go.at[r]))
    pl.semaphore_wait(barrier, len(peers))

    sent = []

    def send(src, dst, here, device):
        i = len(sent)
        copy = pltpu.make_async_remote_copy(
            src, dst, send_sem.at[i], recv_sem.at[i], device, MESH
        )
        copy.start()
        sent.append(copy)
        landing = pltpu.make_async_remote_copy(
            src, here, send_sem.at[i], recv_sem.at[i], device, MESH
        )
        return landing.wait_recv

    share = depth * 3 // 32
    rest = depth // 16

    def rows_of(r, par, cor, d, at, size):
        if par is None:
            start = 8 * share + (cor * 2 + d) * rest
        else:
            start = (par * 4 + cor * 2 + d) * share
        where = pl.ds(pl.multiple_of(start + at, 16), size)
        return w_hbm.at[where] if r == 0 else panel.at[r, where]

    fine, coarse, whole = [(0, 16), (16, share - 16)], [(0, share)], [(0, rest)]
    x_got, z_got, passed = {}, {}, [[], [], [], []]

    def x_send(source, r, shared, d, at, size):
        par = parity if shared else None
        dst = rows_of(r, par, core, d, at, size)
        device = right_x if r == 3 or (r == 2 and d == 0) else left_x
        got = send(rows_of(source, par, core, d, at, size), dst, dst, device)
        x_got.setdefault((r, shared, d), []).append((at, size, got))

    def own_x(shared, d, pieces, r):
        for at, size in pieces:
            x_send(0, r, shared, d, at, size)

    def pass_on(r, par, d, at, size):
        block = rows_of(r, par, core, d, at, size)
        theirs = rows_of(r, par, 1 - core, d, at, size)
        passed[r].append(send(block, block, theirs, sibling))

    def on_x(r, shared, d):
        for at, size, got in x_got[r, shared, d]:
            got()
            if (r, d) == (3, 0) or (r, d) == (1, 1):
                x_send(r, 2, shared, d, at, size)
            if shared:
                block = rows_of(r, parity, core, d, at, size)
                other = rows_of(r, 1 - parity, core, d, at, size)
                got = send(block, block, other, up_z if d == 0 else down_z)
                z_got.setdefault((r, d), []).append((at, size, got))
            pass_on(r, parity if shared else None, d, at, size)

    def on_z(r, d):
        for at, size, got in z_got[r, d]:
            got()
            pass_on(r, 1 - parity, d, at, size)

    def slot_done(r):
        for got in passed[r]:
            got()

    own_x(True, 0, fine, 3)
    own_x(True, 1, fine, 1)
    own_x(True, 1, coarse, 3)
    own_x(True, 0, coarse, 1)

    def part_of(ref, i):
        return ref.at[pl.ds(pl.multiple_of(i * 64, 64), 64)]

    def spread(local, got):
        waits = []
        for o in (4, 5, 3, 6, 2, 7, 1):
            to, source = lax.rem(member + o, 8), lax.rem(member + 8 - o, 8)
            waits.append(
                send(part_of(local, to), part_of(got, member), part_of(got, source), mate(to))
            )
        part_of(got, member)[...] = part_of(local, member)[...]
        return waits

    def totals(waits, got, tot, far):
        for wait in waits:
            wait()
        tot[...] = sum(got[i * 64 : i * 64 + 64].astype(F32) for i in range(8)).astype(BF)
        return [
            send(tot, far.at[o - 1], far.at[o - 1], at_ctx(c + 8 * o))
            for o in range(1, n_groups)
        ]

    def scan(waits, got, far, out, state, reverse):
        running = jnp.zeros((64, DH), F32)
        for o in range(1, n_groups):
            waits[o - 1]()
            earlier = group >= o
            keep = jnp.where(earlier, 0.0, 1.0) if reverse else jnp.where(earlier, 1.0, 0.0)
            running = running + keep.astype(F32) * far[o - 1].astype(F32)
        for i in reversed(range(8)) if reverse else range(8):
            out[i * 64 : i * 64 + 64] = running.astype(BF)
            running = running + got[i * 64 : i * 64 + 64].astype(F32)
        waits = []
        for o in (4, 5, 3, 6, 2, 7, 1):
            to, source = lax.rem(member + o, 8), lax.rem(member + 8 - o, 8)
            waits.append(
                send(part_of(out, to), part_of(state, member), part_of(state, source), mate(to))
            )
        part_of(state, member)[...] = part_of(out, member)[...]
        return waits

    def head(ref, h):
        return ref[:, h * DH : (h + 1) * DH]

    def state_of(ref, h):
        return ref[h * DH : (h + 1) * DH, :]

    first = lax.broadcasted_iota(jnp.int32, (rows, rows), 0)
    second = lax.broadcasted_iota(jnp.int32, (rows, rows), 1)
    causal = (first >= second).astype(F32)
    causal_t = (first <= second).astype(F32)

    load_k.wait()
    load_v.wait()
    for h in range(heads):
        local_kv[h * DH : (h + 1) * DH, :] = dot(head(k_ref, h), head(v_ref, h), 0, 0).astype(BF)
    kv_waits = spread(local_kv, got_kv)

    load_q.wait()
    for h in range(heads):
        scores = (dot(head(q_ref, h), head(k_ref, h), 1, 1) * causal).astype(BF)
        attn32[:, h * DH : (h + 1) * DH] = dot(scores, head(v_ref, h), 1, 0)
    load_w.wait()
    load_go[0].wait()

    on_x(3, True, 0)
    on_x(1, True, 1)
    kv_waits = totals(kv_waits, got_kv, tot_kv, far_kv)
    grad_acc[...] = dot(go[0], panel[0], 1, 1)
    on_x(3, True, 1)
    on_x(1, True, 0)
    for d, r in ((0, 3), (1, 1), (1, 3), (0, 1)):
        own_x(False, d, whole, r)
    on_z(3, 0)
    on_z(1, 1)
    kv_waits = scan(kv_waits, got_kv, far_kv, out_kv, prefix, False)
    on_x(2, True, 0)
    on_x(2, True, 1)
    on_z(3, 1)
    on_z(1, 0)
    on_x(3, False, 0)
    on_x(1, False, 1)
    for wait in kv_waits:
        wait()
    for h in range(heads):
        total = attn32[:, h * DH : (h + 1) * DH] + dot(head(q_ref, h), state_of(prefix, h), 1, 0)
        attn16[:, h * DH : (h + 1) * DH] = (factor * total).astype(BF)

    half = wide // 4

    def project(r):
        for i in range(4):
            part[r * 4 + i] = dot(
                attn16[...], panel[r, :, i * half : (i + 1) * half], 1, 0
            ).astype(BF)

    on_x(3, False, 1)
    on_x(1, False, 0)
    project(0)
    on_z(2, 0)
    on_z(2, 1)
    for r in (3, 1):
        slot_done(r)
        load_go[r].wait()
        grad_acc[...] += dot(go[r], panel[r], 1, 1)
        if r == 3:
            on_x(2, False, 0)
            on_x(2, False, 1)
        project(r)
    slot_done(2)
    load_go[2].wait()

    def chunk_of(to, which):
        slot = lax.rem(to // 2 + n_x - x, n_x)
        return slot * 4 + lax.rem(to, 2) * 2 + which

    distance = (4, 3, 3, 2, 2, 1, 1)
    y_got = ([], [])

    def y_step(j):
        for way in range(2):
            to = lax.rem(y + (distance[j] if way == 0 else n_y - distance[j]), n_y)
            chunk = chunk_of(to, (j + way) % 2)
            if j >= 2:
                y_got[way][j - 2]()
                total = part[chunk].astype(F32) + y_in[way * 7 + j - 2].astype(F32)
                part[chunk] = total.astype(BF)
            landing = y_in.at[way * 7 + j]
            y_got[way].append(
                send(part.at[chunk], landing, landing, up_y if way == 0 else down_y)
            )

    project(2)
    y_step(0)
    y_step(1)
    grads = (grad_acc[...] + dot(go[2], panel[2], 1, 1)).astype(BF)
    g_heads = [grads[:, h * DH : (h + 1) * DH] for h in range(heads)]
    for h in range(heads):
        local_qd[h * DH : (h + 1) * DH, :] = dot(head(q_ref, h), g_heads[h], 0, 0).astype(BF)
    qd_waits = spread(local_qd, got_qd)
    for h in range(heads):
        own = slice(h * DH, (h + 1) * DH)
        d_scores = (dot(g_heads[h], head(v_ref, h), 1, 1) * causal).astype(BF)
        total = dot(d_scores, head(k_ref, h), 1, 0) + dot(g_heads[h], state_of(prefix, h), 1, 1)
        dq_ref[0, :, own] = (factor * total).astype(BF)
    y_step(2)
    qd_waits = totals(qd_waits, got_qd, tot_qd, far_qd)
    y_step(3)
    for h in range(heads):
        own = slice(h * DH, (h + 1) * DH)
        d_scores = (dot(head(v_ref, h), g_heads[h], 1, 1) * causal_t).astype(BF)
        attn32[:, own] = dot(d_scores, head(q_ref, h), 1, 0)
        scores = (dot(head(k_ref, h), head(q_ref, h), 1, 1) * causal_t).astype(BF)
        grad_acc[:, own] = dot(scores, g_heads[h], 1, 0)
    y_step(4)
    qd_waits = scan(qd_waits, got_qd, far_qd, out_qd, suffix, True)
    y_step(5)
    y_step(6)
    for wait in qd_waits:
        wait()
    for h in range(heads):
        own = slice(h * DH, (h + 1) * DH)
        total = attn32[:, own] + dot(head(v_ref, h), state_of(suffix, h), 1, 1)
        dk_ref[0, :, own] = (factor * total).astype(BF)
        total = grad_acc[:, own] + dot(head(k_ref, h), state_of(suffix, h), 1, 0)
        dv_ref[0, :, own] = (factor * total).astype(BF)
    for which in range(2):
        up, down = 6 - which, 5 + which
        y_got[0][up]()
        y_got[1][down]()
        total = part[chunk_of(y, which)].astype(F32)
        total = total + y_in[up].astype(F32) + y_in[7 + down].astype(F32)
        att_ref[0, :, which * half : (which + 1) * half] = total.astype(BF)
    for copy in sent:
        copy.wait_send()


def hand_over(*refs):
    n = len(refs) // 2
    copies = [pltpu.make_async_copy(refs[i], refs[n + i], refs[-1].at[i]) for i in range(n)]
    for copy in copies:
        copy.start()
    for copy in copies:
        copy.wait()


def solution(mesh):
    n_ctx, n_x, n_y = mesh.shape["context"], mesh.shape["dp"], mesh.shape["tensor"]

    def shards(q, k, v, w, go):
        _, rows, width = q.shape
        depth, wide = w.shape
        factor = float(DH * rows * n_ctx) ** (-0.5)
        states = width // DH * DH
        half = wide // 4
        sizes = (n_ctx, n_x, n_y, factor)
        head_out = jax.ShapeDtypeStruct((1, rows, width), BF)
        state = pltpu.VMEM((states, DH), BF)
        total = pltpu.VMEM((states // 8, DH), BF)
        far = pltpu.VMEM((2, states // 8, DH), BF)
        results = (
            jax.ShapeDtypeStruct((1, rows, n_x * wide // n_y), BF),
            head_out,
            head_out,
            head_out,
        )
        ready = pl.pallas_call(
            functools.partial(kernel, sizes),
            out_shape=results,
            in_specs=[pl.BlockSpec(memory_space=pl.ANY)] * 5,
            out_specs=[pl.BlockSpec(memory_space=pltpu.VMEM)] * 4,
            scratch_shapes=[
                pltpu.VMEM((rows, width), BF),
                pltpu.VMEM((rows, width), BF),
                pltpu.VMEM((rows, width), BF),
                pltpu.VMEM((n_x, depth, wide), BF),
                pltpu.VMEM((n_x, rows, wide), BF),
                pltpu.VMEM((rows, width), F32),
                pltpu.VMEM((rows, width), F32),
                pltpu.VMEM((rows, width), BF),
                pltpu.VMEM((4 * n_x, rows, half), BF),
                pltpu.VMEM((14, rows, half), BF),
                state, state, state, state, total, total, far, far,
                state, state, state, state,
                pltpu.SemaphoreType.DMA((98,)),
                pltpu.SemaphoreType.DMA((98,)),
                pltpu.SemaphoreType.DMA((8,)),
            ],
            compiler_params=pltpu.CompilerParams(
                collective_id=0, has_side_effects=True, vmem_limit_bytes=56 << 20
            ),
        )(q, k, v, w, go)
        return pl.pallas_call(
            hand_over,
            out_shape=results,
            in_specs=[pl.BlockSpec(memory_space=pl.ANY)] * 4,
            out_specs=[pl.BlockSpec(memory_space=pl.ANY)] * 4,
            scratch_shapes=[pltpu.SemaphoreType.DMA((4,))],
        )(*ready)

    rows_spec = P("dp", "context", "tensor")
    return jax.shard_map(
        shards,
        mesh=mesh,
        in_specs=(rows_spec, rows_spec, rows_spec, P("tensor", "dp"), P("dp", "context", None)),
        out_specs=(rows_spec,) * 4,
        check_vma=False,
    )
```

```python
import functools

import jax
import jax.numpy as jnp
from jax import lax
from jax.experimental import pallas as pl
from jax.experimental.pallas import tpu as pltpu
from jax.sharding import PartitionSpec as P

DH = 128
BF = jnp.bfloat16
F32 = jnp.float32
MESH = pl.DeviceIdType.MESH


def dot(a, b, ca, cb):
    return lax.dot_general(a, b, (((ca,), (cb,)), ((), ())), preferred_element_type=F32)


def kernel(
    sizes, q_hbm, k_hbm, v_hbm, w_hbm, go_hbm, att_ref, dq_ref, dk_ref, dv_ref,
    q_ref, k_ref, v_ref, panel, go, grad_acc, attn32, attn16, part, y_in,
    local_kv, local_qd, got_kv, got_qd, tot_kv, tot_qd, far_kv, far_qd,
    out_kv, out_qd, prefix, suffix, send_sem, recv_sem, load_sem,
):
    n_ctx, n_x, n_y, factor = sizes
    rows, width = q_ref.shape
    heads = width // DH
    depth, wide = panel.shape[1:]
    c, x, y = lax.axis_index("context"), lax.axis_index("dp"), lax.axis_index("tensor")
    core, z = lax.rem(c, 2), c // 2
    parity = lax.rem(z, 2)
    member, group = lax.rem(c, 8), c // 8
    n_groups = n_ctx // 8

    def at_ctx(i):
        return {"context": lax.rem(i + n_ctx, n_ctx)}

    right_x, left_x = {"dp": lax.rem(x + 1, n_x)}, {"dp": lax.rem(x + n_x - 1, n_x)}
    up_y, down_y = {"tensor": lax.rem(y + 1, n_y)}, {"tensor": lax.rem(y + n_y - 1, n_y)}
    up_z, down_z = at_ctx(c + 2), at_ctx(c - 2)
    sibling = {"context": c + 1 - 2 * core}

    def mate(i):
        return {"context": c - member + i}

    barrier = pltpu.get_barrier_semaphore()
    peers = [right_x, left_x, up_y, down_y, up_z, down_z]
    peers += [mate(lax.rem(member + o, 8)) for o in range(1, 8)]
    peers += [at_ctx(c + 8 * o) for o in range(1, n_groups)]
    for peer in peers:
        pl.semaphore_signal(barrier, inc=1, device_id=peer, device_id_type=MESH)

    loads = []

    def load(src, dst):
        copy = pltpu.make_async_copy(src, dst, load_sem.at[len(loads)])
        copy.start()
        loads.append(copy)
        return copy

    load_k = load(k_hbm.at[0], k_ref)
    load_v = load(v_hbm.at[0], v_ref)
    load_q = load(q_hbm.at[0], q_ref)
    load_w = load(w_hbm, panel.at[0])
    load_go = []
    for r in range(n_x):
        columns = pl.ds(pl.multiple_of(lax.rem(x + r, n_x) * wide, wide), wide)
        load_go.append(load(go_hbm.at[0, :, columns], go.at[r]))
    pl.semaphore_wait(barrier, len(peers))

    sent = []

    def send(src, dst, here, device):
        i = len(sent)
        copy = pltpu.make_async_remote_copy(
            src, dst, send_sem.at[i], recv_sem.at[i], device, MESH
        )
        copy.start()
        sent.append(copy)
        landing = pltpu.make_async_remote_copy(
            src, here, send_sem.at[i], recv_sem.at[i], device, MESH
        )
        return landing.wait_recv

    share = depth * 3 // 32
    rest = depth // 16

    def rows_of(r, par, cor, d, at, size):
        if par is None:
            start = 8 * share + (cor * 2 + d) * rest
        else:
            start = (par * 4 + cor * 2 + d) * share
        where = pl.ds(pl.multiple_of(start + at, 16), size)
        return w_hbm.at[where] if r == 0 else panel.at[r, where]

    fine, coarse, whole = [(0, 16), (16, share - 16)], [(0, share)], [(0, rest)]
    x_got, z_got, passed = {}, {}, [[], [], [], []]

    def x_send(source, r, shared, d, at, size):
        par = parity if shared else None
        dst = rows_of(r, par, core, d, at, size)
        device = right_x if r == 3 or (r == 2 and d == 0) else left_x
        got = send(rows_of(source, par, core, d, at, size), dst, dst, device)
        x_got.setdefault((r, shared, d), []).append((at, size, got))

    def own_x(shared, d, pieces, r):
        for at, size in pieces:
            x_send(0, r, shared, d, at, size)

    def pass_on(r, par, d, at, size):
        block = rows_of(r, par, core, d, at, size)
        theirs = rows_of(r, par, 1 - core, d, at, size)
        passed[r].append(send(block, block, theirs, sibling))

    def on_x(r, shared, d):
        for at, size, got in x_got[r, shared, d]:
            got()
            if (r, d) == (3, 0) or (r, d) == (1, 1):
                x_send(r, 2, shared, d, at, size)
            if shared:
                block = rows_of(r, parity, core, d, at, size)
                other = rows_of(r, 1 - parity, core, d, at, size)
                got = send(block, block, other, up_z if d == 0 else down_z)
                z_got.setdefault((r, d), []).append((at, size, got))
            pass_on(r, parity if shared else None, d, at, size)

    def on_z(r, d):
        for at, size, got in z_got[r, d]:
            got()
            pass_on(r, 1 - parity, d, at, size)

    def slot_done(r):
        for got in passed[r]:
            got()

    own_x(True, 0, fine, 3)
    own_x(True, 1, fine, 1)
    own_x(True, 1, coarse, 3)
    own_x(True, 0, coarse, 1)

    def part_of(ref, i):
        return ref.at[pl.ds(pl.multiple_of(i * 64, 64), 64)]

    def spread(local, got):
        waits = []
        for o in (4, 5, 3, 6, 2, 7, 1):
            to, source = lax.rem(member + o, 8), lax.rem(member + 8 - o, 8)
            waits.append(
                send(part_of(local, to), part_of(got, member), part_of(got, source), mate(to))
            )
        part_of(got, member)[...] = part_of(local, member)[...]
        return waits

    def totals(waits, got, tot, far):
        for wait in waits:
            wait()
        tot[...] = sum(got[i * 64 : i * 64 + 64].astype(F32) for i in range(8)).astype(BF)
        return [
            send(tot, far.at[o - 1], far.at[o - 1], at_ctx(c + 8 * o))
            for o in range(1, n_groups)
        ]

    def scan(waits, got, far, out, state, reverse):
        running = jnp.zeros((64, DH), F32)
        for o in range(1, n_groups):
            waits[o - 1]()
            earlier = group >= o
            keep = jnp.where(earlier, 0.0, 1.0) if reverse else jnp.where(earlier, 1.0, 0.0)
            running = running + keep.astype(F32) * far[o - 1].astype(F32)
        for i in reversed(range(8)) if reverse else range(8):
            out[i * 64 : i * 64 + 64] = running.astype(BF)
            running = running + got[i * 64 : i * 64 + 64].astype(F32)
        waits = []
        for o in (4, 5, 3, 6, 2, 7, 1):
            to, source = lax.rem(member + o, 8), lax.rem(member + 8 - o, 8)
            waits.append(
                send(part_of(out, to), part_of(state, member), part_of(state, source), mate(to))
            )
        part_of(state, member)[...] = part_of(out, member)[...]
        return waits

    def head(ref, h):
        return ref[:, h * DH : (h + 1) * DH]

    def state_of(ref, h):
        return ref[h * DH : (h + 1) * DH, :]

    first = lax.broadcasted_iota(jnp.int32, (rows, rows), 0)
    second = lax.broadcasted_iota(jnp.int32, (rows, rows), 1)
    causal = (first >= second).astype(F32)
    causal_t = (first <= second).astype(F32)

    load_k.wait()
    load_v.wait()
    for h in range(heads):
        local_kv[h * DH : (h + 1) * DH, :] = dot(head(k_ref, h), head(v_ref, h), 0, 0).astype(BF)
    kv_waits = spread(local_kv, got_kv)

    load_q.wait()
    for h in range(heads):
        scores = (dot(head(q_ref, h), head(k_ref, h), 1, 1) * causal).astype(BF)
        attn32[:, h * DH : (h + 1) * DH] = dot(scores, head(v_ref, h), 1, 0)
    load_w.wait()
    load_go[0].wait()

    on_x(3, True, 0)
    on_x(1, True, 1)
    kv_waits = totals(kv_waits, got_kv, tot_kv, far_kv)
    grad_acc[...] = dot(go[0], panel[0], 1, 1)
    on_x(3, True, 1)
    on_x(1, True, 0)
    for d, r in ((0, 3), (1, 1), (1, 3), (0, 1)):
        own_x(False, d, whole, r)
    on_z(3, 0)
    on_z(1, 1)
    kv_waits = scan(kv_waits, got_kv, far_kv, out_kv, prefix, False)
    on_x(2, True, 0)
    on_x(2, True, 1)
    on_z(3, 1)
    on_z(1, 0)
    on_x(3, False, 0)
    on_x(1, False, 1)
    for wait in kv_waits:
        wait()
    for h in range(heads):
        total = attn32[:, h * DH : (h + 1) * DH] + dot(head(q_ref, h), state_of(prefix, h), 1, 0)
        attn16[:, h * DH : (h + 1) * DH] = (factor * total).astype(BF)

    half = wide // 4

    def project(r):
        for i in range(4):
            part[r * 4 + i] = dot(
                attn16[...], panel[r, :, i * half : (i + 1) * half], 1, 0
            ).astype(BF)

    on_x(3, False, 1)
    on_x(1, False, 0)
    project(0)
    on_z(2, 0)
    on_z(2, 1)
    for r in (3, 1):
        slot_done(r)
        load_go[r].wait()
        grad_acc[...] += dot(go[r], panel[r], 1, 1)
        if r == 3:
            on_x(2, False, 0)
            on_x(2, False, 1)
        project(r)
    slot_done(2)
    load_go[2].wait()

    def chunk_of(to, which):
        slot = lax.rem(to // 2 + n_x - x, n_x)
        return slot * 4 + lax.rem(to, 2) * 2 + which

    distance = (4, 3, 3, 2, 2, 1, 1)
    y_got = ([], [])

    def y_step(j):
        for way in range(2):
            to = lax.rem(y + (distance[j] if way == 0 else n_y - distance[j]), n_y)
            chunk = chunk_of(to, (j + way) % 2)
            if j >= 2:
                y_got[way][j - 2]()
                total = part[chunk].astype(F32) + y_in[way * 7 + j - 2].astype(F32)
                part[chunk] = total.astype(BF)
            landing = y_in.at[way * 7 + j]
            y_got[way].append(
                send(part.at[chunk], landing, landing, up_y if way == 0 else down_y)
            )

    project(2)
    y_step(0)
    y_step(1)
    grads = (grad_acc[...] + dot(go[2], panel[2], 1, 1)).astype(BF)
    g_heads = [grads[:, h * DH : (h + 1) * DH] for h in range(heads)]
    for h in range(heads):
        local_qd[h * DH : (h + 1) * DH, :] = dot(head(q_ref, h), g_heads[h], 0, 0).astype(BF)
    qd_waits = spread(local_qd, got_qd)
    for h in range(heads):
        own = slice(h * DH, (h + 1) * DH)
        d_scores = (dot(g_heads[h], head(v_ref, h), 1, 1) * causal).astype(BF)
        total = dot(d_scores, head(k_ref, h), 1, 0) + dot(g_heads[h], state_of(prefix, h), 1, 1)
        dq_ref[0, :, own] = (factor * total).astype(BF)
    y_step(2)
    qd_waits = totals(qd_waits, got_qd, tot_qd, far_qd)
    y_step(3)
    for h in range(heads):
        own = slice(h * DH, (h + 1) * DH)
        d_scores = (dot(head(v_ref, h), g_heads[h], 1, 1) * causal_t).astype(BF)
        attn32[:, own] = dot(d_scores, head(q_ref, h), 1, 0)
        scores = (dot(head(k_ref, h), head(q_ref, h), 1, 1) * causal_t).astype(BF)
        grad_acc[:, own] = dot(scores, g_heads[h], 1, 0)
    y_step(4)
    qd_waits = scan(qd_waits, got_qd, far_qd, out_qd, suffix, True)
    y_step(5)
    y_step(6)
    for wait in qd_waits:
        wait()
    for h in range(heads):
        own = slice(h * DH, (h + 1) * DH)
        total = attn32[:, own] + dot(head(v_ref, h), state_of(suffix, h), 1, 1)
        dk_ref[0, :, own] = (factor * total).astype(BF)
        total = grad_acc[:, own] + dot(head(k_ref, h), state_of(suffix, h), 1, 0)
        dv_ref[0, :, own] = (factor * total).astype(BF)
    for which in range(2):
        up, down = 6 - which, 5 + which
        y_got[0][up]()
        y_got[1][down]()
        total = part[chunk_of(y, which)].astype(F32)
        total = total + y_in[up].astype(F32) + y_in[7 + down].astype(F32)
        att_ref[0, :, which * half : (which + 1) * half] = total.astype(BF)
    for copy in sent:
        copy.wait_send()


def hand_over(*refs):
    n = len(refs) // 2
    copies = [pltpu.make_async_copy(refs[i], refs[n + i], refs[-1].at[i]) for i in range(n)]
    for copy in copies:
        copy.start()
    for copy in copies:
        copy.wait()


def solution(mesh):
    n_ctx, n_x, n_y = mesh.shape["context"], mesh.shape["dp"], mesh.shape["tensor"]

    def shards(q, k, v, w, go):
        _, rows, width = q.shape
        depth, wide = w.shape
        factor = float(DH * rows * n_ctx) ** (-0.5)
        states = width // DH * DH
        half = wide // 4
        sizes = (n_ctx, n_x, n_y, factor)
        head_out = jax.ShapeDtypeStruct((1, rows, width), BF)
        state = pltpu.VMEM((states, DH), BF)
        total = pltpu.VMEM((states // 8, DH), BF)
        far = pltpu.VMEM((2, states // 8, DH), BF)
        results = (
            jax.ShapeDtypeStruct((1, rows, n_x * wide // n_y), BF),
            head_out,
            head_out,
            head_out,
        )
        ready = pl.pallas_call(
            functools.partial(kernel, sizes),
            out_shape=results,
            in_specs=[pl.BlockSpec(memory_space=pltpu.HBM)] * 5,
            out_specs=[pl.BlockSpec(memory_space=pltpu.VMEM)] * 4,
            scratch_shapes=[
                pltpu.VMEM((rows, width), BF),
                pltpu.VMEM((rows, width), BF),
                pltpu.VMEM((rows, width), BF),
                pltpu.VMEM((n_x, depth, wide), BF),
                pltpu.VMEM((n_x, rows, wide), BF),
                pltpu.VMEM((rows, width), F32),
                pltpu.VMEM((rows, width), F32),
                pltpu.VMEM((rows, width), BF),
                pltpu.VMEM((4 * n_x, rows, half), BF),
                pltpu.VMEM((14, rows, half), BF),
                state, state, state, state, total, total, far, far,
                state, state, state, state,
                pltpu.SemaphoreType.DMA((98,)),
                pltpu.SemaphoreType.DMA((98,)),
                pltpu.SemaphoreType.DMA((8,)),
            ],
            compiler_params=pltpu.CompilerParams(
                collective_id=0, has_side_effects=True, vmem_limit_bytes=54784 << 10
            ),
        )(q, k, v, w, go)
        return pl.pallas_call(
            hand_over,
            out_shape=results,
            in_specs=[pl.BlockSpec(memory_space=pl.ANY)] * 4,
            out_specs=[pl.BlockSpec(memory_space=pl.ANY)] * 4,
            scratch_shapes=[pltpu.SemaphoreType.DMA((4,))],
            compiler_params=pltpu.CompilerParams(vmem_limit_bytes=1 << 20),
        )(*ready)

    rows_spec = P("dp", "context", "tensor")
    return jax.shard_map(
        shards,
        mesh=mesh,
        in_specs=(rows_spec, rows_spec, rows_spec, P("tensor", "dp"), P("dp", "context", None)),
        out_specs=(rows_spec,) * 4,
        check_vma=False,
    )
```

```python
import functools

import jax
import jax.numpy as jnp
from jax import lax
from jax.experimental import pallas as pl
from jax.experimental.pallas import tpu as pltpu
from jax.sharding import PartitionSpec as P

DH = 128
BF = jnp.bfloat16
F32 = jnp.float32
MESH = pl.DeviceIdType.MESH


def dot(a, b, ca, cb):
    return lax.dot_general(a, b, (((ca,), (cb,)), ((), ())), preferred_element_type=F32)


def kernel(
    sizes, q_hbm, k_hbm, v_hbm, w_hbm, go_hbm, att_ref, dq_ref, dk_ref, dv_ref,
    q_ref, k_ref, v_ref, panel, go, grad_acc, attn32, attn16, part, y_in,
    local_kv, local_qd, got_kv, got_qd, tot_kv, tot_qd, far_kv, far_qd,
    out_kv, out_qd, prefix, suffix, send_sem, recv_sem, load_sem, gate,
):
    n_ctx, n_x, n_y, factor = sizes
    rows, width = q_ref.shape
    heads = width // DH
    depth, wide = panel.shape[1:]
    c, x, y = lax.axis_index("context"), lax.axis_index("dp"), lax.axis_index("tensor")
    core, z = lax.rem(c, 2), c // 2
    parity = lax.rem(z, 2)
    member, group = lax.rem(c, 8), c // 8
    n_groups = n_ctx // 8

    def at_ctx(i):
        return {"context": lax.rem(i + n_ctx, n_ctx)}

    right_x, left_x = {"dp": lax.rem(x + 1, n_x)}, {"dp": lax.rem(x + n_x - 1, n_x)}
    up_y, down_y = {"tensor": lax.rem(y + 1, n_y)}, {"tensor": lax.rem(y + n_y - 1, n_y)}
    up_z, down_z = at_ctx(c + 2), at_ctx(c - 2)
    sibling = {"context": c + 1 - 2 * core}

    def mate(i):
        return {"context": c - member + i}

    barrier = pltpu.get_barrier_semaphore()
    peers = [right_x, left_x, up_y, down_y, up_z, down_z]
    peers += [mate(lax.rem(member + o, 8)) for o in range(1, 8)]
    for peer in peers:
        pl.semaphore_signal(barrier, inc=1, device_id=peer, device_id_type=MESH)

    loads = []

    def load(src, dst):
        copy = pltpu.make_async_copy(src, dst, load_sem.at[len(loads)])
        copy.start()
        loads.append(copy)
        return copy

    load_k = load(k_hbm.at[0], k_ref)
    load_v = load(v_hbm.at[0], v_ref)
    load_q = load(q_hbm.at[0], q_ref)
    load_w = load(w_hbm, panel.at[0])
    load_go = []
    for r in range(n_x):
        columns = pl.ds(pl.multiple_of(lax.rem(x + r, n_x) * wide, wide), wide)
        load_go.append(load(go_hbm.at[0, :, columns], go.at[r]))
    pl.semaphore_wait(barrier, len(peers))

    def signal(i, device):
        pl.semaphore_signal(gate.at[i], inc=1, device_id=device, device_id_type=MESH)

    @pl.when(member == 0)
    def _():
        signal(0, down_z)

    @pl.when(member == 6)
    def _():
        signal(0, up_z)

    def greet():
        for i, end in ((1, 0), (2, 6)):

            @pl.when(member == end)
            def _():
                pl.semaphore_wait(gate.at[0], 1)
                for o in range(1, 8):
                    signal(i, mate(lax.rem(member + o, 8)))

    def greeted():
        for i, end in ((1, 0), (2, 6)):

            @pl.when(member != end)
            def _():
                pl.semaphore_wait(gate.at[i], 1)

    sent = []

    def send(src, dst, here, device):
        i = len(sent)
        copy = pltpu.make_async_remote_copy(
            src, dst, send_sem.at[i], recv_sem.at[i], device, MESH
        )
        copy.start()
        sent.append(copy)
        landing = pltpu.make_async_remote_copy(
            src, here, send_sem.at[i], recv_sem.at[i], device, MESH
        )
        return landing.wait_recv

    share = depth * 3 // 32
    rest = depth // 16

    def rows_of(r, par, cor, d, at, size):
        if par is None:
            start = 8 * share + (cor * 2 + d) * rest
        else:
            start = (par * 4 + cor * 2 + d) * share
        where = pl.ds(pl.multiple_of(start + at, 16), size)
        return w_hbm.at[where] if r == 0 else panel.at[r, where]

    fine, coarse, whole = [(0, 16), (16, share - 16)], [(0, share)], [(0, rest)]
    x_got, z_got, passed = {}, {}, [[], [], [], []]

    def x_send(source, r, shared, d, at, size):
        par = parity if shared else None
        dst = rows_of(r, par, core, d, at, size)
        device = right_x if r == 3 or (r == 2 and d == 0) else left_x
        got = send(rows_of(source, par, core, d, at, size), dst, dst, device)
        x_got.setdefault((r, shared, d), []).append((at, size, got))

    def own_x(shared, d, pieces, r):
        for at, size in pieces:
            x_send(0, r, shared, d, at, size)

    def pass_on(r, par, d, at, size):
        block = rows_of(r, par, core, d, at, size)
        theirs = rows_of(r, par, 1 - core, d, at, size)
        passed[r].append(send(block, block, theirs, sibling))

    def on_x(r, shared, d):
        for at, size, got in x_got[r, shared, d]:
            got()
            if (r, d) == (3, 0) or (r, d) == (1, 1):
                x_send(r, 2, shared, d, at, size)
            if shared:
                block = rows_of(r, parity, core, d, at, size)
                other = rows_of(r, 1 - parity, core, d, at, size)
                got = send(block, block, other, up_z if d == 0 else down_z)
                z_got.setdefault((r, d), []).append((at, size, got))
            pass_on(r, parity if shared else None, d, at, size)

    def on_z(r, d):
        for at, size, got in z_got[r, d]:
            got()
            pass_on(r, 1 - parity, d, at, size)

    def slot_done(r):
        for got in passed[r]:
            got()

    own_x(True, 0, fine, 3)
    own_x(True, 1, fine, 1)
    own_x(True, 1, coarse, 3)
    own_x(True, 0, coarse, 1)

    def part_of(ref, i):
        return ref.at[pl.ds(pl.multiple_of(i * 64, 64), 64)]

    def spread(local, got):
        waits = []
        for o in (4, 5, 3, 6, 2, 7, 1):
            to, source = lax.rem(member + o, 8), lax.rem(member + 8 - o, 8)
            waits.append(
                send(part_of(local, to), part_of(got, member), part_of(got, source), mate(to))
            )
        part_of(got, member)[...] = part_of(local, member)[...]
        return waits

    def totals(waits, got, tot, far):
        for wait in waits:
            wait()
        tot[...] = sum(got[i * 64 : i * 64 + 64].astype(F32) for i in range(8)).astype(BF)
        return [
            send(tot, far.at[o - 1], far.at[o - 1], at_ctx(c + 8 * o))
            for o in range(1, n_groups)
        ]

    def scan(waits, got, far, out, state, reverse):
        running = jnp.zeros((64, DH), F32)
        for o in range(1, n_groups):
            waits[o - 1]()
            earlier = group >= o
            keep = jnp.where(earlier, 0.0, 1.0) if reverse else jnp.where(earlier, 1.0, 0.0)
            running = running + keep.astype(F32) * far[o - 1].astype(F32)
        for i in reversed(range(8)) if reverse else range(8):
            out[i * 64 : i * 64 + 64] = running.astype(BF)
            running = running + got[i * 64 : i * 64 + 64].astype(F32)
        waits = []
        for o in (4, 5, 3, 6, 2, 7, 1):
            to, source = lax.rem(member + o, 8), lax.rem(member + 8 - o, 8)
            waits.append(
                send(part_of(out, to), part_of(state, member), part_of(state, source), mate(to))
            )
        part_of(state, member)[...] = part_of(out, member)[...]
        return waits

    def head(ref, h):
        return ref[:, h * DH : (h + 1) * DH]

    def state_of(ref, h):
        return ref[h * DH : (h + 1) * DH, :]

    first = lax.broadcasted_iota(jnp.int32, (rows, rows), 0)
    second = lax.broadcasted_iota(jnp.int32, (rows, rows), 1)
    causal = (first >= second).astype(F32)
    causal_t = (first <= second).astype(F32)

    load_k.wait()
    load_v.wait()
    for h in range(heads):
        local_kv[h * DH : (h + 1) * DH, :] = dot(head(k_ref, h), head(v_ref, h), 0, 0).astype(BF)
    kv_waits = spread(local_kv, got_kv)

    load_q.wait()
    for h in range(heads):
        scores = (dot(head(q_ref, h), head(k_ref, h), 1, 1) * causal).astype(BF)
        attn32[:, h * DH : (h + 1) * DH] = dot(scores, head(v_ref, h), 1, 0)
    greet()
    load_w.wait()
    load_go[0].wait()

    on_x(3, True, 0)
    on_x(1, True, 1)
    greeted()
    kv_waits = totals(kv_waits, got_kv, tot_kv, far_kv)
    grad_acc[...] = dot(go[0], panel[0], 1, 1)
    on_x(3, True, 1)
    on_x(1, True, 0)
    for d, r in ((0, 3), (1, 1), (1, 3), (0, 1)):
        own_x(False, d, whole, r)
    on_z(3, 0)
    on_z(1, 1)
    kv_waits = scan(kv_waits, got_kv, far_kv, out_kv, prefix, False)
    on_x(2, True, 0)
    on_x(2, True, 1)
    on_z(3, 1)
    on_z(1, 0)
    on_x(3, False, 0)
    on_x(1, False, 1)
    for wait in kv_waits:
        wait()
    for h in range(heads):
        total = attn32[:, h * DH : (h + 1) * DH] + dot(head(q_ref, h), state_of(prefix, h), 1, 0)
        attn16[:, h * DH : (h + 1) * DH] = (factor * total).astype(BF)

    half = wide // 4

    def project(r):
        for i in range(4):
            part[r * 4 + i] = dot(
                attn16[...], panel[r, :, i * half : (i + 1) * half], 1, 0
            ).astype(BF)

    on_x(3, False, 1)
    on_x(1, False, 0)
    project(0)
    on_z(2, 0)
    on_z(2, 1)
    for r in (3, 1):
        slot_done(r)
        load_go[r].wait()
        grad_acc[...] += dot(go[r], panel[r], 1, 1)
        if r == 3:
            on_x(2, False, 0)
            on_x(2, False, 1)
        project(r)
    slot_done(2)
    load_go[2].wait()

    def chunk_of(to, which):
        slot = lax.rem(to // 2 + n_x - x, n_x)
        return slot * 4 + lax.rem(to, 2) * 2 + which

    distance = (4, 3, 3, 2, 2, 1, 1)
    y_got = ([], [])

    def y_step(j):
        for way in range(2):
            to = lax.rem(y + (distance[j] if way == 0 else n_y - distance[j]), n_y)
            chunk = chunk_of(to, (j + way) % 2)
            if j >= 2:
                y_got[way][j - 2]()
                total = part[chunk].astype(F32) + y_in[way * 7 + j - 2].astype(F32)
                part[chunk] = total.astype(BF)
            landing = y_in.at[way * 7 + j]
            y_got[way].append(
                send(part.at[chunk], landing, landing, up_y if way == 0 else down_y)
            )

    project(2)
    y_step(0)
    y_step(1)
    grads = (grad_acc[...] + dot(go[2], panel[2], 1, 1)).astype(BF)
    g_heads = [grads[:, h * DH : (h + 1) * DH] for h in range(heads)]
    for h in range(heads):
        local_qd[h * DH : (h + 1) * DH, :] = dot(head(q_ref, h), g_heads[h], 0, 0).astype(BF)
    qd_waits = spread(local_qd, got_qd)
    for h in range(heads):
        own = slice(h * DH, (h + 1) * DH)
        d_scores = (dot(g_heads[h], head(v_ref, h), 1, 1) * causal).astype(BF)
        total = dot(d_scores, head(k_ref, h), 1, 0) + dot(g_heads[h], state_of(prefix, h), 1, 1)
        dq_ref[0, :, own] = (factor * total).astype(BF)
    y_step(2)
    y_step(3)
    qd_waits = totals(qd_waits, got_qd, tot_qd, far_qd)
    for h in range(heads):
        own = slice(h * DH, (h + 1) * DH)
        d_scores = (dot(head(v_ref, h), g_heads[h], 1, 1) * causal_t).astype(BF)
        attn32[:, own] = dot(d_scores, head(q_ref, h), 1, 0)
        scores = (dot(head(k_ref, h), head(q_ref, h), 1, 1) * causal_t).astype(BF)
        grad_acc[:, own] = dot(scores, g_heads[h], 1, 0)
    y_step(4)
    y_step(5)
    qd_waits = scan(qd_waits, got_qd, far_qd, out_qd, suffix, True)
    y_step(6)
    for wait in qd_waits:
        wait()
    for h in range(heads):
        own = slice(h * DH, (h + 1) * DH)
        total = attn32[:, own] + dot(head(v_ref, h), state_of(suffix, h), 1, 1)
        dk_ref[0, :, own] = (factor * total).astype(BF)
        total = grad_acc[:, own] + dot(head(k_ref, h), state_of(suffix, h), 1, 0)
        dv_ref[0, :, own] = (factor * total).astype(BF)
    for which in range(2):
        up, down = 6 - which, 5 + which
        y_got[0][up]()
        y_got[1][down]()
        total = part[chunk_of(y, which)].astype(F32)
        total = total + y_in[up].astype(F32) + y_in[7 + down].astype(F32)
        att_ref[0, :, which * half : (which + 1) * half] = total.astype(BF)
    for copy in sent:
        copy.wait_send()


def hand_over(*refs):
    n = len(refs) // 2
    copies = [pltpu.make_async_copy(refs[i], refs[n + i], refs[-1].at[i]) for i in range(n)]
    for copy in copies:
        copy.start()
    for copy in copies:
        copy.wait()


def solution(mesh):
    n_ctx, n_x, n_y = mesh.shape["context"], mesh.shape["dp"], mesh.shape["tensor"]

    def shards(q, k, v, w, go):
        _, rows, width = q.shape
        depth, wide = w.shape
        factor = float(DH * rows * n_ctx) ** (-0.5)
        states = width // DH * DH
        half = wide // 4
        sizes = (n_ctx, n_x, n_y, factor)
        head_out = jax.ShapeDtypeStruct((1, rows, width), BF)
        state = pltpu.VMEM((states, DH), BF)
        total = pltpu.VMEM((states // 8, DH), BF)
        far = pltpu.VMEM((2, states // 8, DH), BF)
        results = (
            jax.ShapeDtypeStruct((1, rows, n_x * wide // n_y), BF),
            head_out,
            head_out,
            head_out,
        )
        ready = pl.pallas_call(
            functools.partial(kernel, sizes),
            out_shape=results,
            in_specs=[pl.BlockSpec(memory_space=pltpu.HBM)] * 5,
            out_specs=[pl.BlockSpec(memory_space=pltpu.VMEM)] * 4,
            scratch_shapes=[
                pltpu.VMEM((rows, width), BF),
                pltpu.VMEM((rows, width), BF),
                pltpu.VMEM((rows, width), BF),
                pltpu.VMEM((n_x, depth, wide), BF),
                pltpu.VMEM((n_x, rows, wide), BF),
                pltpu.VMEM((rows, width), F32),
                pltpu.VMEM((rows, width), F32),
                pltpu.VMEM((rows, width), BF),
                pltpu.VMEM((4 * n_x, rows, half), BF),
                pltpu.VMEM((14, rows, half), BF),
                state, state, state, state, total, total, far, far,
                state, state, state, state,
                pltpu.SemaphoreType.DMA((98,)),
                pltpu.SemaphoreType.DMA((98,)),
                pltpu.SemaphoreType.DMA((8,)),
                pltpu.SemaphoreType.REGULAR((3,)),
            ],
            compiler_params=pltpu.CompilerParams(
                collective_id=0, has_side_effects=True, vmem_limit_bytes=54784 << 10
            ),
        )(q, k, v, w, go)
        return pl.pallas_call(
            hand_over,
            out_shape=results,
            in_specs=[pl.BlockSpec(memory_space=pl.ANY)] * 4,
            out_specs=[pl.BlockSpec(memory_space=pl.ANY)] * 4,
            scratch_shapes=[pltpu.SemaphoreType.DMA((4,))],
            compiler_params=pltpu.CompilerParams(vmem_limit_bytes=1 << 20),
        )(*ready)

    rows_spec = P("dp", "context", "tensor")
    return jax.shard_map(
        shards,
        mesh=mesh,
        in_specs=(rows_spec, rows_spec, rows_spec, P("tensor", "dp"), P("dp", "context", None)),
        out_specs=(rows_spec,) * 4,
        check_vma=False,
    )
```

```python
import functools

import jax
import jax.numpy as jnp
from jax import lax
from jax.experimental import pallas as pl
from jax.experimental.pallas import tpu as pltpu
from jax.sharding import PartitionSpec as P

DH = 128
BF = jnp.bfloat16
F32 = jnp.float32
MESH = pl.DeviceIdType.MESH


def dot(a, b, ca, cb):
    return lax.dot_general(a, b, (((ca,), (cb,)), ((), ())), preferred_element_type=F32)


def kernel(
    sizes, q_hbm, k_hbm, v_hbm, w_hbm, go_hbm, att_ref, dq_ref, dk_ref, dv_ref,
    q_ref, k_ref, v_ref, panel, go, grad_acc, attn32, attn16, part, y_in,
    local_kv, local_qd, got_kv, got_qd, tot_kv, tot_qd, far_kv, far_qd,
    out_kv, out_qd, prefix, suffix, send_sem, recv_sem, load_sem, gate,
):
    n_ctx, n_x, n_y, factor = sizes
    rows, width = q_ref.shape
    heads = width // DH
    depth, wide = panel.shape[1:]
    c, x, y = lax.axis_index("context"), lax.axis_index("dp"), lax.axis_index("tensor")
    core, z = lax.rem(c, 2), c // 2
    parity = lax.rem(z, 2)
    member, group = lax.rem(c, 8), c // 8
    n_groups = n_ctx // 8

    def at_ctx(i):
        return {"context": lax.rem(i + n_ctx, n_ctx)}

    right_x, left_x = {"dp": lax.rem(x + 1, n_x)}, {"dp": lax.rem(x + n_x - 1, n_x)}
    up_y, down_y = {"tensor": lax.rem(y + 1, n_y)}, {"tensor": lax.rem(y + n_y - 1, n_y)}
    up_z, down_z = at_ctx(c + 2), at_ctx(c - 2)
    sibling = {"context": c + 1 - 2 * core}

    def mate(i):
        return {"context": c - member + i}

    barrier = pltpu.get_barrier_semaphore()
    peers = [right_x, left_x, up_y, down_y, up_z, down_z]
    peers += [mate(lax.rem(member + o, 8)) for o in range(1, 8)]
    for peer in peers:
        pl.semaphore_signal(barrier, inc=1, device_id=peer, device_id_type=MESH)

    loads = []

    def load(src, dst):
        copy = pltpu.make_async_copy(src, dst, load_sem.at[len(loads)])
        copy.start()
        loads.append(copy)
        return copy

    load_k = load(k_hbm.at[0], k_ref)
    load_v = load(v_hbm.at[0], v_ref)
    load_q = load(q_hbm.at[0], q_ref)
    load_w = load(w_hbm, panel.at[0])
    load_go = []
    for r in range(n_x):
        columns = pl.ds(pl.multiple_of(lax.rem(x + r, n_x) * wide, wide), wide)
        load_go.append(load(go_hbm.at[0, :, columns], go.at[r]))
    pl.semaphore_wait(barrier, len(peers))

    def signal(i, device):
        pl.semaphore_signal(gate.at[i], inc=1, device_id=device, device_id_type=MESH)

    @pl.when(member == 0)
    def _():
        signal(0, down_z)

    @pl.when(member == 6)
    def _():
        signal(0, up_z)

    def greet():
        for i, end in ((1, 0), (2, 6)):

            @pl.when(member == end)
            def _():
                pl.semaphore_wait(gate.at[0], 1)
                for o in range(1, 8):
                    signal(i, mate(lax.rem(member + o, 8)))

    def greeted():
        for i, end in ((1, 0), (2, 6)):

            @pl.when(member != end)
            def _():
                pl.semaphore_wait(gate.at[i], 1)

    sent = []

    def send(src, dst, here, device):
        i = len(sent)
        copy = pltpu.make_async_remote_copy(
            src, dst, send_sem.at[i], recv_sem.at[i], device, MESH
        )
        copy.start()
        sent.append(copy)
        landing = pltpu.make_async_remote_copy(
            src, here, send_sem.at[i], recv_sem.at[i], device, MESH
        )
        return landing.wait_recv

    share = depth * 3 // 32
    rest = depth // 16

    def rows_of(r, par, cor, d, at, size):
        if par is None:
            start = 8 * share + (cor * 2 + d) * rest
        else:
            start = (par * 4 + cor * 2 + d) * share
        where = pl.ds(pl.multiple_of(start + at, 16), size)
        return w_hbm.at[where] if r == 0 else panel.at[r, where]

    fine, coarse, whole = [(0, 16), (16, share - 16)], [(0, share)], [(0, rest)]
    x_got, z_got, passed = {}, {}, [[], [], [], []]

    def x_send(source, r, shared, d, at, size):
        par = parity if shared else None
        dst = rows_of(r, par, core, d, at, size)
        device = right_x if r == 3 or (r == 2 and d == 0) else left_x
        got = send(rows_of(source, par, core, d, at, size), dst, dst, device)
        x_got.setdefault((r, shared, d), []).append((at, size, got))

    def own_x(shared, d, pieces, r):
        for at, size in pieces:
            x_send(0, r, shared, d, at, size)

    def pass_on(r, par, d, at, size):
        block = rows_of(r, par, core, d, at, size)
        theirs = rows_of(r, par, 1 - core, d, at, size)
        passed[r].append(send(block, block, theirs, sibling))

    def on_x(r, shared, d):
        for at, size, got in x_got[r, shared, d]:
            got()
            if (r, d) == (3, 0) or (r, d) == (1, 1):
                x_send(r, 2, shared, d, at, size)
            if shared:
                block = rows_of(r, parity, core, d, at, size)
                other = rows_of(r, 1 - parity, core, d, at, size)
                got = send(block, block, other, up_z if d == 0 else down_z)
                z_got.setdefault((r, d), []).append((at, size, got))
            pass_on(r, parity if shared else None, d, at, size)

    def on_z(r, d):
        for at, size, got in z_got[r, d]:
            got()
            pass_on(r, 1 - parity, d, at, size)

    def slot_done(r):
        for got in passed[r]:
            got()

    own_x(True, 0, fine, 3)
    own_x(True, 1, fine, 1)
    own_x(True, 1, coarse, 3)
    own_x(True, 0, coarse, 1)

    def part_of(ref, i):
        return ref.at[pl.ds(pl.multiple_of(i * 64, 64), 64)]

    def spread(local, got):
        waits = []
        for o in (4, 5, 3, 6, 2, 7, 1):
            to, source = lax.rem(member + o, 8), lax.rem(member + 8 - o, 8)
            waits.append(
                send(part_of(local, to), part_of(got, member), part_of(got, source), mate(to))
            )
        part_of(got, member)[...] = part_of(local, member)[...]
        return waits

    def totals(waits, got, tot, far):
        for wait in waits:
            wait()
        tot[...] = sum(got[i * 64 : i * 64 + 64].astype(F32) for i in range(8)).astype(BF)
        return [
            send(tot, far.at[o - 1], far.at[o - 1], at_ctx(c + 8 * o))
            for o in range(1, n_groups)
        ]

    def scan(waits, got, far, out, state, reverse):
        running = jnp.zeros((64, DH), F32)
        for o in range(1, n_groups):
            waits[o - 1]()
            earlier = group >= o
            keep = jnp.where(earlier, 0.0, 1.0) if reverse else jnp.where(earlier, 1.0, 0.0)
            running = running + keep.astype(F32) * far[o - 1].astype(F32)
        for i in reversed(range(8)) if reverse else range(8):
            out[i * 64 : i * 64 + 64] = running.astype(BF)
            running = running + got[i * 64 : i * 64 + 64].astype(F32)
        waits = []
        for o in (4, 5, 3, 6, 2, 7, 1):
            to, source = lax.rem(member + o, 8), lax.rem(member + 8 - o, 8)
            waits.append(
                send(part_of(out, to), part_of(state, member), part_of(state, source), mate(to))
            )
        part_of(state, member)[...] = part_of(out, member)[...]
        return waits

    def head(ref, h):
        return ref[:, h * DH : (h + 1) * DH]

    def state_of(ref, h):
        return ref[h * DH : (h + 1) * DH, :]

    first = lax.broadcasted_iota(jnp.int32, (rows, rows), 0)
    second = lax.broadcasted_iota(jnp.int32, (rows, rows), 1)
    causal = (first >= second).astype(F32)
    causal_t = (first <= second).astype(F32)

    load_k.wait()
    load_v.wait()
    for h in range(heads):
        local_kv[h * DH : (h + 1) * DH, :] = dot(head(k_ref, h), head(v_ref, h), 0, 0).astype(BF)
    kv_waits = spread(local_kv, got_kv)

    load_q.wait()
    for h in range(heads):
        scores = (dot(head(q_ref, h), head(k_ref, h), 1, 1) * causal).astype(BF)
        attn32[:, h * DH : (h + 1) * DH] = dot(scores, head(v_ref, h), 1, 0)
    greet()
    load_w.wait()
    load_go[0].wait()

    on_x(3, True, 0)
    on_x(1, True, 1)
    greeted()
    kv_waits = totals(kv_waits, got_kv, tot_kv, far_kv)
    grad_acc[...] = dot(go[0], panel[0], 1, 1)
    on_x(3, True, 1)
    on_x(1, True, 0)
    for d, r in ((0, 3), (1, 1), (1, 3), (0, 1)):
        own_x(False, d, whole, r)
    on_z(3, 0)
    on_z(1, 1)
    kv_waits = scan(kv_waits, got_kv, far_kv, out_kv, prefix, False)
    on_x(2, True, 0)
    on_x(2, True, 1)
    on_z(3, 1)
    on_z(1, 0)
    on_x(3, False, 0)
    on_x(1, False, 1)
    for wait in kv_waits:
        wait()
    for h in range(heads):
        total = attn32[:, h * DH : (h + 1) * DH] + dot(head(q_ref, h), state_of(prefix, h), 1, 0)
        attn16[:, h * DH : (h + 1) * DH] = (factor * total).astype(BF)

    half = wide // 4

    def project(r):
        for i in range(4):
            part[r * 4 + i] = dot(
                attn16[...], panel[r, :, i * half : (i + 1) * half], 1, 0
            ).astype(BF)

    on_x(3, False, 1)
    on_x(1, False, 0)
    project(0)
    on_z(2, 0)
    on_z(2, 1)
    slot_done(3)
    project(3)
    on_x(2, False, 0)
    on_x(2, False, 1)
    slot_done(1)
    project(1)
    slot_done(2)
    load_go[2].wait()

    def chunk_of(to, which):
        slot = lax.rem(to // 2 + n_x - x, n_x)
        return slot * 4 + lax.rem(to, 2) * 2 + which

    distance = (4, 3, 3, 2, 2, 1, 1)
    y_got = ([], [])

    def y_step(j):
        for way in range(2):
            to = lax.rem(y + (distance[j] if way == 0 else n_y - distance[j]), n_y)
            chunk = chunk_of(to, (j + way) % 2)
            if j >= 2:
                y_got[way][j - 2]()
                total = part[chunk].astype(F32) + y_in[way * 7 + j - 2].astype(F32)
                part[chunk] = total.astype(BF)
            landing = y_in.at[way * 7 + j]
            y_got[way].append(
                send(part.at[chunk], landing, landing, up_y if way == 0 else down_y)
            )

    project(2)
    y_step(0)
    y_step(1)
    for r in (3, 1):
        load_go[r].wait()
        grad_acc[...] += dot(go[r], panel[r], 1, 1)
    grads = (grad_acc[...] + dot(go[2], panel[2], 1, 1)).astype(BF)
    g_heads = [grads[:, h * DH : (h + 1) * DH] for h in range(heads)]
    for h in range(heads):
        local_qd[h * DH : (h + 1) * DH, :] = dot(head(q_ref, h), g_heads[h], 0, 0).astype(BF)
    qd_waits = spread(local_qd, got_qd)
    for h in range(heads):
        own = slice(h * DH, (h + 1) * DH)
        d_scores = (dot(g_heads[h], head(v_ref, h), 1, 1) * causal).astype(BF)
        total = dot(d_scores, head(k_ref, h), 1, 0) + dot(g_heads[h], state_of(prefix, h), 1, 1)
        dq_ref[0, :, own] = (factor * total).astype(BF)
    y_step(2)
    y_step(3)
    qd_waits = totals(qd_waits, got_qd, tot_qd, far_qd)
    for h in range(heads):
        own = slice(h * DH, (h + 1) * DH)
        d_scores = (dot(head(v_ref, h), g_heads[h], 1, 1) * causal_t).astype(BF)
        attn32[:, own] = dot(d_scores, head(q_ref, h), 1, 0)
        scores = (dot(head(k_ref, h), head(q_ref, h), 1, 1) * causal_t).astype(BF)
        grad_acc[:, own] = dot(scores, g_heads[h], 1, 0)
    y_step(4)
    y_step(5)
    qd_waits = scan(qd_waits, got_qd, far_qd, out_qd, suffix, True)
    y_step(6)
    for wait in qd_waits:
        wait()
    for h in range(heads):
        own = slice(h * DH, (h + 1) * DH)
        total = attn32[:, own] + dot(head(v_ref, h), state_of(suffix, h), 1, 1)
        dk_ref[0, :, own] = (factor * total).astype(BF)
        total = grad_acc[:, own] + dot(head(k_ref, h), state_of(suffix, h), 1, 0)
        dv_ref[0, :, own] = (factor * total).astype(BF)
    for which in range(2):
        up, down = 6 - which, 5 + which
        y_got[0][up]()
        y_got[1][down]()
        total = part[chunk_of(y, which)].astype(F32)
        total = total + y_in[up].astype(F32) + y_in[7 + down].astype(F32)
        att_ref[0, :, which * half : (which + 1) * half] = total.astype(BF)
    for copy in sent:
        copy.wait_send()


def hand_over(*refs):
    n = len(refs) // 2
    copies = [pltpu.make_async_copy(refs[i], refs[n + i], refs[-1].at[i]) for i in range(n)]
    for copy in copies:
        copy.start()
    for copy in copies:
        copy.wait()


def solution(mesh):
    n_ctx, n_x, n_y = mesh.shape["context"], mesh.shape["dp"], mesh.shape["tensor"]

    def shards(q, k, v, w, go):
        _, rows, width = q.shape
        depth, wide = w.shape
        factor = float(DH * rows * n_ctx) ** (-0.5)
        states = width // DH * DH
        half = wide // 4
        sizes = (n_ctx, n_x, n_y, factor)
        head_out = jax.ShapeDtypeStruct((1, rows, width), BF)
        state = pltpu.VMEM((states, DH), BF)
        total = pltpu.VMEM((states // 8, DH), BF)
        far = pltpu.VMEM((2, states // 8, DH), BF)
        results = (
            jax.ShapeDtypeStruct((1, rows, n_x * wide // n_y), BF),
            head_out,
            head_out,
            head_out,
        )
        ready = pl.pallas_call(
            functools.partial(kernel, sizes),
            out_shape=results,
            in_specs=[pl.BlockSpec(memory_space=pltpu.HBM)] * 5,
            out_specs=[pl.BlockSpec(memory_space=pltpu.VMEM)] * 4,
            scratch_shapes=[
                pltpu.VMEM((rows, width), BF),
                pltpu.VMEM((rows, width), BF),
                pltpu.VMEM((rows, width), BF),
                pltpu.VMEM((n_x, depth, wide), BF),
                pltpu.VMEM((n_x, rows, wide), BF),
                pltpu.VMEM((rows, width), F32),
                pltpu.VMEM((rows, width), F32),
                pltpu.VMEM((rows, width), BF),
                pltpu.VMEM((4 * n_x, rows, half), BF),
                pltpu.VMEM((14, rows, half), BF),
                state, state, state, state, total, total, far, far,
                state, state, state, state,
                pltpu.SemaphoreType.DMA((98,)),
                pltpu.SemaphoreType.DMA((98,)),
                pltpu.SemaphoreType.DMA((8,)),
                pltpu.SemaphoreType.REGULAR((3,)),
            ],
            compiler_params=pltpu.CompilerParams(
                collective_id=0, has_side_effects=True, vmem_limit_bytes=54784 << 10
            ),
        )(q, k, v, w, go)
        return pl.pallas_call(
            hand_over,
            out_shape=results,
            in_specs=[pl.BlockSpec(memory_space=pl.ANY)] * 4,
            out_specs=[pl.BlockSpec(memory_space=pl.ANY)] * 4,
            scratch_shapes=[pltpu.SemaphoreType.DMA((4,))],
            compiler_params=pltpu.CompilerParams(vmem_limit_bytes=1 << 20),
        )(*ready)

    rows_spec = P("dp", "context", "tensor")
    return jax.shard_map(
        shards,
        mesh=mesh,
        in_specs=(rows_spec, rows_spec, rows_spec, P("tensor", "dp"), P("dp", "context", None)),
        out_specs=(rows_spec,) * 4,
        check_vma=False,
    )
```

```python
import functools

import jax
import jax.numpy as jnp
from jax import lax
from jax.experimental import pallas as pl
from jax.experimental.pallas import tpu as pltpu
from jax.sharding import PartitionSpec as P

DH = 128
BF = jnp.bfloat16
F32 = jnp.float32
MESH = pl.DeviceIdType.MESH


def dot(a, b, ca, cb):
    return lax.dot_general(a, b, (((ca,), (cb,)), ((), ())), preferred_element_type=F32)


def kernel(
    sizes, q_hbm, k_hbm, v_hbm, w_hbm, go_hbm, att_ref, dq_ref, dk_ref, dv_ref,
    q_ref, k_ref, v_ref, panel, go, grad_acc, attn32, attn16, part, y_in,
    local_kv, local_qd, got_kv, got_qd, tot_kv, tot_qd, far_kv, far_qd,
    out_kv, out_qd, prefix, suffix, send_sem, recv_sem, load_sem, gate,
):
    n_ctx, n_x, n_y, factor = sizes
    rows, width = q_ref.shape
    heads = width // DH
    depth, wide = panel.shape[1:]
    c, x, y = lax.axis_index("context"), lax.axis_index("dp"), lax.axis_index("tensor")
    core, z = lax.rem(c, 2), c // 2
    parity = lax.rem(z, 2)
    member, group = lax.rem(c, 8), c // 8
    n_groups = n_ctx // 8

    def at_ctx(i):
        return {"context": lax.rem(i + n_ctx, n_ctx)}

    right_x, left_x = {"dp": lax.rem(x + 1, n_x)}, {"dp": lax.rem(x + n_x - 1, n_x)}
    up_y, down_y = {"tensor": lax.rem(y + 1, n_y)}, {"tensor": lax.rem(y + n_y - 1, n_y)}
    up_z, down_z = at_ctx(c + 2), at_ctx(c - 2)
    sibling = {"context": c + 1 - 2 * core}

    def mate(i):
        return {"context": c - member + i}

    barrier = pltpu.get_barrier_semaphore()
    peers = [right_x, left_x, up_y, down_y, up_z, down_z]
    peers += [mate(lax.rem(member + o, 8)) for o in range(1, 8)]
    for peer in peers:
        pl.semaphore_signal(barrier, inc=1, device_id=peer, device_id_type=MESH)

    loads = []

    def load(src, dst):
        copy = pltpu.make_async_copy(src, dst, load_sem.at[len(loads)])
        copy.start()
        loads.append(copy)
        return copy

    load_k = load(k_hbm.at[0], k_ref)
    load_v = load(v_hbm.at[0], v_ref)
    pl.semaphore_wait(barrier, len(peers))

    def signal(i, device):
        pl.semaphore_signal(gate.at[i], inc=1, device_id=device, device_id_type=MESH)

    @pl.when(member == 0)
    def _():
        signal(0, down_z)

    @pl.when(member == 6)
    def _():
        signal(0, up_z)

    def greet():
        for i, end in ((1, 0), (2, 6)):

            @pl.when(member == end)
            def _():
                pl.semaphore_wait(gate.at[0], 1)
                for o in range(1, 8):
                    signal(i, mate(lax.rem(member + o, 8)))

    def greeted():
        for i, end in ((1, 0), (2, 6)):

            @pl.when(member != end)
            def _():
                pl.semaphore_wait(gate.at[i], 1)

    sent = []

    def send(src, dst, here, device):
        i = len(sent)
        copy = pltpu.make_async_remote_copy(
            src, dst, send_sem.at[i], recv_sem.at[i], device, MESH
        )
        copy.start()
        sent.append(copy)
        landing = pltpu.make_async_remote_copy(
            src, here, send_sem.at[i], recv_sem.at[i], device, MESH
        )
        return landing.wait_recv

    share = depth * 3 // 32
    rest = depth // 16

    def rows_of(r, par, cor, d, at, size):
        if par is None:
            start = 8 * share + (cor * 2 + d) * rest
        else:
            start = (par * 4 + cor * 2 + d) * share
        where = pl.ds(pl.multiple_of(start + at, 16), size)
        return w_hbm.at[where] if r == 0 else panel.at[r, where]

    fine, coarse, whole = [(0, 16), (16, share - 16)], [(0, share)], [(0, rest)]
    x_got, z_got, passed = {}, {}, [[], [], [], []]

    def x_send(source, r, shared, d, at, size):
        par = parity if shared else None
        dst = rows_of(r, par, core, d, at, size)
        device = right_x if r == 3 or (r == 2 and d == 0) else left_x
        got = send(rows_of(source, par, core, d, at, size), dst, dst, device)
        x_got.setdefault((r, shared, d), []).append((at, size, got))

    def own_x(shared, d, pieces, r):
        for at, size in pieces:
            x_send(0, r, shared, d, at, size)

    def pass_on(r, par, d, at, size):
        block = rows_of(r, par, core, d, at, size)
        theirs = rows_of(r, par, 1 - core, d, at, size)
        passed[r].append(send(block, block, theirs, sibling))

    def on_x(r, shared, d):
        for at, size, got in x_got[r, shared, d]:
            got()
            if (r, d) == (3, 0) or (r, d) == (1, 1):
                x_send(r, 2, shared, d, at, size)
            if shared:
                block = rows_of(r, parity, core, d, at, size)
                other = rows_of(r, 1 - parity, core, d, at, size)
                got = send(block, block, other, up_z if d == 0 else down_z)
                z_got.setdefault((r, d), []).append((at, size, got))
            pass_on(r, parity if shared else None, d, at, size)

    def on_z(r, d):
        for at, size, got in z_got[r, d]:
            got()
            pass_on(r, 1 - parity, d, at, size)

    def slot_done(r):
        for got in passed[r]:
            got()

    own_x(True, 0, fine, 3)
    own_x(True, 1, fine, 1)
    own_x(True, 1, coarse, 3)
    own_x(True, 0, coarse, 1)

    load_q = load(q_hbm.at[0], q_ref)
    load_w = load(w_hbm, panel.at[0])
    load_go = []
    for r in range(n_x):
        columns = pl.ds(pl.multiple_of(lax.rem(x + r, n_x) * wide, wide), wide)
        load_go.append(load(go_hbm.at[0, :, columns], go.at[r]))

    def part_of(ref, i):
        return ref.at[pl.ds(pl.multiple_of(i * 64, 64), 64)]

    def spread(local, got):
        waits = []
        for o in (4, 5, 3, 6, 2, 7, 1):
            to, source = lax.rem(member + o, 8), lax.rem(member + 8 - o, 8)
            waits.append(
                send(part_of(local, to), part_of(got, member), part_of(got, source), mate(to))
            )
        part_of(got, member)[...] = part_of(local, member)[...]
        return waits

    def totals(waits, got, tot, far):
        for wait in waits:
            wait()
        tot[...] = sum(got[i * 64 : i * 64 + 64].astype(F32) for i in range(8)).astype(BF)
        return [
            send(tot, far.at[o - 1], far.at[o - 1], at_ctx(c + 8 * o))
            for o in range(1, n_groups)
        ]

    def scan(waits, got, far, out, state, reverse):
        running = jnp.zeros((64, DH), F32)
        for o in range(1, n_groups):
            waits[o - 1]()
            earlier = group >= o
            keep = jnp.where(earlier, 0.0, 1.0) if reverse else jnp.where(earlier, 1.0, 0.0)
            running = running + keep.astype(F32) * far[o - 1].astype(F32)
        for i in reversed(range(8)) if reverse else range(8):
            out[i * 64 : i * 64 + 64] = running.astype(BF)
            running = running + got[i * 64 : i * 64 + 64].astype(F32)
        waits = []
        for o in (4, 5, 3, 6, 2, 7, 1):
            to, source = lax.rem(member + o, 8), lax.rem(member + 8 - o, 8)
            waits.append(
                send(part_of(out, to), part_of(state, member), part_of(state, source), mate(to))
            )
        part_of(state, member)[...] = part_of(out, member)[...]
        return waits

    def head(ref, h):
        return ref[:, h * DH : (h + 1) * DH]

    def state_of(ref, h):
        return ref[h * DH : (h + 1) * DH, :]

    first = lax.broadcasted_iota(jnp.int32, (rows, rows), 0)
    second = lax.broadcasted_iota(jnp.int32, (rows, rows), 1)
    causal = (first >= second).astype(F32)
    causal_t = (first <= second).astype(F32)

    load_k.wait()
    load_v.wait()
    for h in range(heads):
        local_kv[h * DH : (h + 1) * DH, :] = dot(head(k_ref, h), head(v_ref, h), 0, 0).astype(BF)
    kv_waits = spread(local_kv, got_kv)

    load_q.wait()
    for h in range(heads):
        scores = (dot(head(q_ref, h), head(k_ref, h), 1, 1) * causal).astype(BF)
        attn32[:, h * DH : (h + 1) * DH] = dot(scores, head(v_ref, h), 1, 0)
    greet()
    load_w.wait()
    load_go[0].wait()

    on_x(3, True, 0)
    on_x(1, True, 1)
    greeted()
    kv_waits = totals(kv_waits, got_kv, tot_kv, far_kv)
    grad_acc[...] = dot(go[0], panel[0], 1, 1)
    on_x(3, True, 1)
    on_x(1, True, 0)
    for d, r in ((0, 3), (1, 1), (1, 3), (0, 1)):
        own_x(False, d, whole, r)
    on_z(3, 0)
    on_z(1, 1)
    kv_waits = scan(kv_waits, got_kv, far_kv, out_kv, prefix, False)
    on_x(2, True, 0)
    on_x(2, True, 1)
    on_z(3, 1)
    on_z(1, 0)
    on_x(3, False, 0)
    on_x(1, False, 1)
    for wait in kv_waits:
        wait()
    for h in range(heads):
        total = attn32[:, h * DH : (h + 1) * DH] + dot(head(q_ref, h), state_of(prefix, h), 1, 0)
        attn16[:, h * DH : (h + 1) * DH] = (factor * total).astype(BF)

    half = wide // 4

    def project(r):
        for i in range(4):
            part[r * 4 + i] = dot(
                attn16[...], panel[r, :, i * half : (i + 1) * half], 1, 0
            ).astype(BF)

    on_x(3, False, 1)
    on_x(1, False, 0)
    project(0)
    on_z(2, 0)
    on_z(2, 1)
    for r in (3, 1):
        slot_done(r)
        load_go[r].wait()
        grad_acc[...] += dot(go[r], panel[r], 1, 1)
        if r == 3:
            on_x(2, False, 0)
            on_x(2, False, 1)
        project(r)
    slot_done(2)
    load_go[2].wait()

    def chunk_of(to, which):
        slot = lax.rem(to // 2 + n_x - x, n_x)
        return slot * 4 + lax.rem(to, 2) * 2 + which

    distance = (4, 3, 3, 2, 2, 1, 1)
    y_got = ([], [])

    def y_step(j):
        for way in range(2):
            to = lax.rem(y + (distance[j] if way == 0 else n_y - distance[j]), n_y)
            chunk = chunk_of(to, (j + way) % 2)
            if j >= 2:
                y_got[way][j - 2]()
                total = part[chunk].astype(F32) + y_in[way * 7 + j - 2].astype(F32)
                part[chunk] = total.astype(BF)
            landing = y_in.at[way * 7 + j]
            y_got[way].append(
                send(part.at[chunk], landing, landing, up_y if way == 0 else down_y)
            )

    project(2)
    y_step(0)
    y_step(1)
    grads = (grad_acc[...] + dot(go[2], panel[2], 1, 1)).astype(BF)
    g_heads = [grads[:, h * DH : (h + 1) * DH] for h in range(heads)]
    for h in range(heads):
        local_qd[h * DH : (h + 1) * DH, :] = dot(head(q_ref, h), g_heads[h], 0, 0).astype(BF)
    qd_waits = spread(local_qd, got_qd)
    for h in range(heads):
        own = slice(h * DH, (h + 1) * DH)
        d_scores = (dot(g_heads[h], head(v_ref, h), 1, 1) * causal).astype(BF)
        total = dot(d_scores, head(k_ref, h), 1, 0) + dot(g_heads[h], state_of(prefix, h), 1, 1)
        dq_ref[0, :, own] = (factor * total).astype(BF)
    y_step(2)
    y_step(3)
    qd_waits = totals(qd_waits, got_qd, tot_qd, far_qd)
    for h in range(heads):
        own = slice(h * DH, (h + 1) * DH)
        d_scores = (dot(head(v_ref, h), g_heads[h], 1, 1) * causal_t).astype(BF)
        attn32[:, own] = dot(d_scores, head(q_ref, h), 1, 0)
        scores = (dot(head(k_ref, h), head(q_ref, h), 1, 1) * causal_t).astype(BF)
        grad_acc[:, own] = dot(scores, g_heads[h], 1, 0)
    y_step(4)
    y_step(5)
    qd_waits = scan(qd_waits, got_qd, far_qd, out_qd, suffix, True)
    y_step(6)
    for wait in qd_waits:
        wait()
    for h in range(heads):
        own = slice(h * DH, (h + 1) * DH)
        total = attn32[:, own] + dot(head(v_ref, h), state_of(suffix, h), 1, 1)
        dk_ref[0, :, own] = (factor * total).astype(BF)
        total = grad_acc[:, own] + dot(head(k_ref, h), state_of(suffix, h), 1, 0)
        dv_ref[0, :, own] = (factor * total).astype(BF)
    for which in range(2):
        up, down = 6 - which, 5 + which
        y_got[0][up]()
        y_got[1][down]()
        total = part[chunk_of(y, which)].astype(F32)
        total = total + y_in[up].astype(F32) + y_in[7 + down].astype(F32)
        att_ref[0, :, which * half : (which + 1) * half] = total.astype(BF)
    for copy in sent:
        copy.wait_send()


def hand_over(*refs):
    n = len(refs) // 2
    copies = [pltpu.make_async_copy(refs[i], refs[n + i], refs[-1].at[i]) for i in range(n)]
    for copy in copies:
        copy.start()
    for copy in copies:
        copy.wait()


def solution(mesh):
    n_ctx, n_x, n_y = mesh.shape["context"], mesh.shape["dp"], mesh.shape["tensor"]

    def shards(q, k, v, w, go):
        _, rows, width = q.shape
        depth, wide = w.shape
        factor = float(DH * rows * n_ctx) ** (-0.5)
        states = width // DH * DH
        half = wide // 4
        sizes = (n_ctx, n_x, n_y, factor)
        head_out = jax.ShapeDtypeStruct((1, rows, width), BF)
        state = pltpu.VMEM((states, DH), BF)
        total = pltpu.VMEM((states // 8, DH), BF)
        far = pltpu.VMEM((2, states // 8, DH), BF)
        results = (
            jax.ShapeDtypeStruct((1, rows, n_x * wide // n_y), BF),
            head_out,
            head_out,
            head_out,
        )
        ready = pl.pallas_call(
            functools.partial(kernel, sizes),
            out_shape=results,
            in_specs=[pl.BlockSpec(memory_space=pltpu.HBM)] * 5,
            out_specs=[pl.BlockSpec(memory_space=pltpu.VMEM)] * 4,
            scratch_shapes=[
                pltpu.VMEM((rows, width), BF),
                pltpu.VMEM((rows, width), BF),
                pltpu.VMEM((rows, width), BF),
                pltpu.VMEM((n_x, depth, wide), BF),
                pltpu.VMEM((n_x, rows, wide), BF),
                pltpu.VMEM((rows, width), F32),
                pltpu.VMEM((rows, width), F32),
                pltpu.VMEM((rows, width), BF),
                pltpu.VMEM((4 * n_x, rows, half), BF),
                pltpu.VMEM((14, rows, half), BF),
                state, state, state, state, total, total, far, far,
                state, state, state, state,
                pltpu.SemaphoreType.DMA((98,)),
                pltpu.SemaphoreType.DMA((98,)),
                pltpu.SemaphoreType.DMA((8,)),
                pltpu.SemaphoreType.REGULAR((3,)),
            ],
            compiler_params=pltpu.CompilerParams(
                collective_id=0, has_side_effects=True, vmem_limit_bytes=54784 << 10
            ),
        )(q, k, v, w, go)
        return pl.pallas_call(
            hand_over,
            out_shape=results,
            in_specs=[pl.BlockSpec(memory_space=pl.ANY)] * 4,
            out_specs=[pl.BlockSpec(memory_space=pl.ANY)] * 4,
            scratch_shapes=[pltpu.SemaphoreType.DMA((4,))],
            compiler_params=pltpu.CompilerParams(vmem_limit_bytes=1 << 20),
        )(*ready)

    rows_spec = P("dp", "context", "tensor")
    return jax.shard_map(
        shards,
        mesh=mesh,
        in_specs=(rows_spec, rows_spec, rows_spec, P("tensor", "dp"), P("dp", "context", None)),
        out_specs=(rows_spec,) * 4,
        check_vma=False,
    )
```
